32 devices in a mesh: row: 8 (over z, x), col: 4 (over y, core).
Axes of the slice: x: 2, y: 2, z: 4, core: 2. Of those that a mesh axis runs over, the one named last changes fastest.
Arguments:
- tensor: bfloat16 [2048, 512, 128], P('row', 'col'), may hold values from -96 to 96
- factor_a: float32 [2048, 128], P(('row', 'col')), may hold values from -4.5 to 4.5
- factor_b: float32 [512, 128], P(('col', 'row')), may hold values from -4.5 to 4.5
- factor_c: float32 [128, 128], replicated, may hold values from -4.5 to 4.5
Outputs:
- new_a: float32 [2048, 128], P(('row', 'col'))
- new_b: float32 [512, 128], P(('col', 'row'))
- new_c: float32 [128, 128], replicated
The draws below stay inside these ranges and needn't reach their ends.
All inputs are finite; a program needn't handle non-finite values.
Results may differ from the reference program's by a relative error of at most 0.01.
Values may be sent and summed in bfloat16 or wider, within the bound.
No kernel may reach another device: no remote copies, remote signals or barrier semaphores. Data moves between devices by JAX's collectives and lax.ppermute only.
A program may use at most 128 MiB of HBM per device.

```python
import jax
import jax.numpy as jnp
from jax import lax

I_DEV = 256
K = 128
R = 128
STEPS = 2
I = 2048
J = 512


def factor_draw(key, salt, row_count):
    folded = jax.random.fold_in(key, salt)
    key_values, key_spread = jax.random.split(folded)
    position = jnp.arange(row_count, dtype=jnp.float32) / (row_count - 1)
    spread = jnp.exp(jax.random.uniform(key_spread, (row_count, 1), jnp.float32, 0.0, 2.3025851))
    values = jnp.clip(jax.random.normal(key_values, (row_count, R), jnp.float32), -3.0, 3.0) * 0.05
    trend = jnp.exp(0.5493061 * position)
    return (values * spread * trend[:, None]).astype(jnp.float32)


def draw_factor_a(key, part):
    return factor_draw(key, 11, I)


def draw_factor_b(key, part):
    return factor_draw(key, 23, J)


def draw_factor_c(key, part):
    return factor_draw(key, 37, K)


def draw_tensor(key, part):
    folded = jax.random.fold_in(key, 7)
    key_values = jax.random.fold_in(folded, 0)
    values = jnp.clip(jax.random.normal(key_values, (I, J, K), jnp.float32), -6.0, 6.0) * 16.0
    return values.astype(jnp.bfloat16)


def setup_inputs(seed: int = 0) -> dict:
    seeds = jax.random.split(jax.random.key(seed), 5)
    tensor = draw_tensor(jax.random.fold_in(seeds[4], 71), 0)
    factor_a = draw_factor_a(jax.random.fold_in(seeds[4], 71), 0)
    factor_b = draw_factor_b(jax.random.fold_in(seeds[4], 71), 0)
    factor_c = draw_factor_c(jax.random.fold_in(seeds[4], 71), 0)
    return dict(tensor=tensor, factor_a=factor_a, factor_b=factor_b, factor_c=factor_c)


damping = 0.9
scaling = 0.25
epsilon = 1e-6


def column_squares(values16):
    return jnp.sum(jnp.square(values16.astype(jnp.float32)), axis=0)


def local_terms(block, tile_a, tile_b, c16):
    rows_i, rows_j, depth = block.shape
    a16 = tile_a.astype(jnp.bfloat16)
    b16 = tile_b.astype(jnp.bfloat16)
    rank = a16.shape[1]
    pairs = (a16.astype(jnp.float32)[:, None, :] * b16.astype(jnp.float32)[None, :, :]).astype(jnp.bfloat16)
    pairs = pairs.reshape(rows_i * rows_j, rank)
    model = jnp.dot(pairs, c16.T, preferred_element_type=jnp.float32)
    resid = (block.reshape(rows_i * rows_j, depth).astype(jnp.float32) - model).astype(jnp.bfloat16)
    along = jnp.dot(resid, c16, preferred_element_type=jnp.float32).reshape(rows_i, rows_j, rank)
    grad_a = jnp.sum(along * b16.astype(jnp.float32)[None, :, :], axis=1)
    grad_b = jnp.sum(along * a16.astype(jnp.float32)[:, None, :], axis=0)
    grad_c = lax.dot_general(resid, pairs, (((0,), (0,)), ((), ())), preferred_element_type=jnp.float32)
    return grad_a, grad_b, grad_c


def reference(tensor, factor_a, factor_b, factor_c):
    rows_i, rows_j, depth = tensor.shape
    rank = factor_a.shape[1]
    blocks = tensor.reshape(rows_i // I_DEV, I_DEV, rows_j, depth)
    current_a, current_b, current_c = factor_a, factor_b, factor_c
    for step in range(STEPS):
        c16 = current_c.astype(jnp.bfloat16)
        norm_a = column_squares(current_a.astype(jnp.bfloat16))
        norm_b = column_squares(current_b.astype(jnp.bfloat16))
        norm_c = column_squares(c16)
        step_a = scaling / (norm_b * norm_c + epsilon)
        step_b = scaling / (norm_a * norm_c + epsilon)
        step_c = scaling / (norm_a * norm_b + epsilon)
        a_blocks = current_a.reshape(rows_i // I_DEV, I_DEV, rank)
        fixed_b = current_b

        def one_block(carry, inputs):
            block, tile_a = inputs
            grad_a, grad_b, grad_c = local_terms(block, tile_a, fixed_b, c16)
            return (carry[0] + grad_b, carry[1] + grad_c), grad_a

        start = (jnp.zeros((rows_j, rank), jnp.float32), jnp.zeros((depth, rank), jnp.float32))
        (total_b, total_c), parts_a = lax.scan(one_block, start, (blocks, a_blocks))
        total_a = parts_a.reshape(rows_i, rank)
        current_a = damping * current_a + step_a * total_a
        current_b = damping * current_b + step_b * total_b
        current_c = damping * current_c + step_c * total_c
    return current_a, current_b, current_c
```

```python
import functools

import jax
import jax.numpy as jnp
from jax import lax
from jax.experimental import pallas as pl
from jax.experimental.pallas import tpu as pltpu
from jax.sharding import PartitionSpec as P

STEPS = 2
F32 = jnp.float32
BF16 = jnp.bfloat16
NORM_ROWS = 16
VMEM_LIMIT = 32 << 20


damping = 0.9
scaling = 0.25
epsilon = 1e-06


def vmem(x):
    return pltpu.with_memory_space_constraint(x, pltpu.VMEM)


def call(body, out_shapes, *operands, hbm_out=False):
    whole = pl.BlockSpec(memory_space=pltpu.VMEM)
    outs = [jax.ShapeDtypeStruct(s, d) if hbm_out else pltpu.VMEM(s, d) for s, d in out_shapes]
    return pl.pallas_call(
        body,
        in_specs=[whole] * len(operands),
        out_specs=[whole] * len(outs),
        out_shape=outs,
        compiler_params=pltpu.CompilerParams(vmem_limit_bytes=VMEM_LIMIT),
    )(*[vmem(x) for x in operands])


def dot(x, y):
    return jnp.dot(x, y, preferred_element_type=F32)


def dot_rows(x, y):
    return lax.dot_general(x, y, (((0,), (0,)), ((), ())), preferred_element_type=F32)


def dot_wide(x16, y):
    high = y.astype(BF16)
    low = (y - high.astype(F32)).astype(BF16)
    return dot(x16, high) + dot(x16, low)


def put_norm(ref, start, norm):
    high = norm.astype(BF16).astype(F32)
    rest = norm - high
    mid = rest.astype(BF16).astype(F32)
    low = rest - mid
    rows = jnp.concatenate([high, mid, low, jnp.zeros((NORM_ROWS - 3, norm.shape[1]), F32)], 0)
    ref[start : start + NORM_ROWS] = rows.astype(BF16)


def get_norm(block):
    rows = block.astype(F32)
    return rows[0:1] + rows[1:2] + rows[2:3]


def squares(x16):
    return jnp.sum(jnp.square(x16.astype(F32)), axis=0, keepdims=True)


def terms_kernel(group, t_ref, a_ref, b_ref, c_ref, col_ref, row_ref, acc_a, acc_b, acc_c):
    rows_i, rows_j, depth = t_ref.shape
    rank = a_ref.shape[1]
    half = group // 2
    b16 = b_ref[...].astype(BF16)
    c16 = c_ref[...].astype(BF16)
    b32 = b16.astype(F32)
    zero = jnp.zeros((depth, rank), BF16)
    twice = jnp.concatenate(
        [jnp.concatenate([c16, zero], 1), jnp.concatenate([zero, c16], 1)], 0
    )
    acc_b[...] = jnp.zeros_like(acc_b)
    acc_c[...] = jnp.zeros_like(acc_c)

    def step(g, carry):
        first = pl.multiple_of(g * group, group)
        block = t_ref[pl.ds(first, group)]
        a16 = a_ref[pl.ds(first, group)].astype(BF16)
        a32 = a16.astype(F32)
        left = block[:half].reshape(half * rows_j, depth)
        right = block[half:].reshape(half * rows_j, depth)
        along = dot(jnp.concatenate([left, right], 1), twice)
        along = jnp.concatenate(
            [along[:, :rank].reshape(half, rows_j, rank), along[:, rank:].reshape(half, rows_j, rank)], 0
        )
        acc_a[pl.ds(first, group)] = jnp.sum(along * b32[None], axis=1)
        total = acc_b[...]
        for q in range(group):
            total = total + along[q] * a32[q : q + 1]
        acc_b[...] = total
        pairs = jnp.concatenate([a16[q : q + 1] * b16 for q in range(group)], 0)
        acc_c[...] += dot_rows(block.reshape(group * rows_j, depth), pairs)
        return carry

    lax.fori_loop(0, rows_i // group, step, 0)
    a16 = a_ref[...].astype(BF16)
    gram_a = dot_rows(a16, a16)
    gram_b = dot_rows(b16, b16)
    gram_c = dot_rows(c16, c16)
    col_ref[:rows_i] = (acc_a[...] - dot_wide(a16, gram_b * gram_c)).astype(BF16)
    col_ref[rows_i : rows_i + depth] = (acc_c[...] - dot_wide(c16, gram_a * gram_b)).astype(BF16)
    put_norm(col_ref, rows_i + depth, squares(b16))
    row_ref[:rows_j] = (acc_b[...] - dot_wide(b16, gram_a * gram_c)).astype(BF16)
    put_norm(row_ref, rows_j, squares(a16))


def local_terms(block, a, b, c):
    rows_i, rows_j, depth = block.shape
    rank = a.shape[1]
    group = next(g for g in (64, 32, 16, 8, 4, 2) if rows_i % g == 0)
    whole = pl.BlockSpec(memory_space=pltpu.VMEM)
    return pl.pallas_call(
        functools.partial(terms_kernel, group),
        in_specs=[whole] * 4,
        out_specs=[whole] * 2,
        out_shape=[
            pltpu.VMEM((rows_i + depth + NORM_ROWS, rank), BF16),
            pltpu.VMEM((rows_j + NORM_ROWS, rank), BF16),
        ],
        scratch_shapes=[
            pltpu.VMEM((rows_i, rank), F32),
            pltpu.VMEM((rows_j, rank), F32),
            pltpu.VMEM((depth, rank), F32),
        ],
        compiler_params=pltpu.CompilerParams(vmem_limit_bytes=VMEM_LIMIT),
    )(vmem(block), vmem(a), vmem(b), vmem(c))


def add_kernel(norm_at, x_ref, y_ref, o_ref):
    o_ref[...] = (x_ref[...].astype(F32) + y_ref[...].astype(F32)).astype(BF16)
    at = slice(norm_at, norm_at + NORM_ROWS)
    put_norm(o_ref, norm_at, get_norm(x_ref[at]) + get_norm(y_ref[at]))


def exchange_sum(x, axis, norm_at):
    n = lax.axis_size(axis)
    d = 1
    while d < n:
        y = lax.ppermute(x, axis, [(i, i ^ d) for i in range(n)])
        (x,) = call(functools.partial(add_kernel, norm_at), [(x.shape, BF16)], x, y)
        d *= 2
    return x


def update_kernel(col_ref, row_ref, a_ref, b_ref, c_ref, new_a, new_b, new_c):
    rows_i, rows_j, depth = a_ref.shape[0], b_ref.shape[0], c_ref.shape[0]
    norm_b = get_norm(col_ref[rows_i + depth :])
    norm_a = get_norm(row_ref[rows_j : rows_j + NORM_ROWS])
    norm_c = squares(c_ref[...].astype(BF16))
    step_a = scaling / (norm_b * norm_c + epsilon)
    step_b = scaling / (norm_a * norm_c + epsilon)
    step_c = scaling / (norm_a * norm_b + epsilon)
    new_a[...] = damping * a_ref[...] + step_a * col_ref[:rows_i].astype(F32)
    new_b[...] = damping * b_ref[...] + step_b * row_ref[:rows_j].astype(F32)
    new_c[...] = damping * c_ref[...] + step_c * row_ref[rows_j + NORM_ROWS :].astype(F32)


def local(tensor, factor_a, factor_b, factor_c):
    rows_i, rows_j, depth = tensor.shape
    own_i, rank = factor_a.shape
    own_j = factor_b.shape[0]
    n_row = lax.axis_size("row")
    tensor = vmem(tensor)
    spread = jnp.broadcast_to(factor_b[None], (n_row, own_j, rank))
    b = lax.all_to_all(spread, "row", 0, 0).reshape(rows_j, rank)
    a = lax.all_gather(factor_a, "col", axis=0, tiled=True)
    c = factor_c
    for step in range(STEPS):
        to_col, to_row = local_terms(tensor, a, b, c)
        to_col = exchange_sum(to_col, "col", rows_i + depth)
        to_row = jnp.concatenate([to_row, to_col[rows_i : rows_i + depth]], 0)
        to_row = exchange_sum(to_row, "row", rows_j)
        a, b, c = call(
            update_kernel,
            [(a.shape, F32), (b.shape, F32), (c.shape, F32)],
            to_col, to_row, a, b, c,
        )
    new_a = lax.dynamic_slice_in_dim(a, lax.axis_index("col") * own_i, own_i, 0)
    new_b = lax.dynamic_slice_in_dim(b, lax.axis_index("row") * own_j, own_j, 0)
    return (new_a, new_b, c)


def solution(mesh):
    return jax.shard_map(
        local,
        mesh=mesh,
        in_specs=(P("row", "col", None), P(("row", "col"), None), P(("col", "row"), None), P()),
        out_specs=(P(("row", "col"), None), P(("col", "row"), None), P()),
        check_vma=False,
    )
```

```python
import functools

import jax
import jax.numpy as jnp
from jax import lax
from jax.experimental import pallas as pl
from jax.experimental.pallas import tpu as pltpu
from jax.sharding import PartitionSpec as P

F32 = jnp.float32
BF16 = jnp.bfloat16
NORM_ROWS = 16
VMEM_LIMIT = 24 << 20
PLACE_FLOPS = 4 * 10**9


damping = 0.9
scaling = 0.25
epsilon = 1e-06


def vmem(x):
    return pltpu.with_memory_space_constraint(x, pltpu.VMEM)


def call(body, outs, *operands, scratch=(), hbm_out=False, flops=0):
    whole = pl.BlockSpec(memory_space=pltpu.VMEM)
    place = jax.ShapeDtypeStruct if hbm_out else pltpu.VMEM
    return pl.pallas_call(
        body,
        in_specs=[whole] * len(operands),
        out_specs=[whole] * len(outs),
        out_shape=[place(s, d) for s, d in outs],
        scratch_shapes=scratch,
        cost_estimate=pl.CostEstimate(flops=flops, bytes_accessed=0, transcendentals=0),
        compiler_params=pltpu.CompilerParams(vmem_limit_bytes=VMEM_LIMIT),
    )(*[vmem(x) for x in operands])


def divisor(n, most):
    return next(g for g in (64, 32, 16, 8, 4, 2) if g <= most and n % g == 0)


def dot(x, y):
    return jnp.dot(x, y, preferred_element_type=F32)


def dot_rows(x, y):
    return lax.dot_general(x, y, (((0,), (0,)), ((), ())), preferred_element_type=F32)


def gram(x16):
    return dot_rows(x16, x16)


def dot_wide(x16, y):
    high = y.astype(BF16)
    low = (y - high.astype(F32)).astype(BF16)
    return dot(x16, high) + dot(x16, low)


def put_norm(ref, start, norm):
    high = norm.astype(BF16).astype(F32)
    rest = norm - high
    mid = rest.astype(BF16).astype(F32)
    low = rest - mid
    rows = jnp.concatenate([high, mid, low, jnp.zeros((NORM_ROWS - 3, norm.shape[1]), F32)], 0)
    ref[start : start + NORM_ROWS] = rows.astype(BF16)


def get_norm(ref, start):
    rows = ref[start : start + NORM_ROWS].astype(F32)
    return rows[0:1] + rows[1:2] + rows[2:3]


def squares(x16):
    return jnp.sum(jnp.square(x16.astype(F32)), axis=0, keepdims=True)


def tree(parts):
    while len(parts) > 1:
        parts = [parts[q] + parts[q + 1] for q in range(0, len(parts), 2)]
    return parts[0]


def sum_rows(refs, start, rows):
    return tree([r[start : start + rows].astype(F32) for r in refs])


def sum_norm(refs, start):
    return tree([get_norm(r, start) for r in refs])


def digits(n):
    weight = 1
    while weight < n:
        radix = 4 if (n // weight) % 4 == 0 else 2
        yield weight, radix
        weight *= radix


def digit_of(axis, weight, radix):
    return lax.rem(lax.div(lax.axis_index(axis), weight), radix)


def swap(x, axis, weight, q):
    return lax.ppermute(x, axis, [(i, i ^ (q * weight)) for i in range(lax.axis_size(axis))])


def twice(c16):
    zero = jnp.zeros_like(c16)
    return jnp.concatenate(
        [jnp.concatenate([c16, zero], 1), jnp.concatenate([zero, c16], 1)], 0
    )


def times_c(block, pair_c):
    group, rows_j, depth = block.shape
    rank = pair_c.shape[1] // 2
    half = group // 2
    left = block[:half].reshape(half * rows_j, depth)
    right = block[half:].reshape(half * rows_j, depth)
    out = dot(jnp.concatenate([left, right], 1), pair_c)
    return jnp.concatenate(
        [out[:, :rank].reshape(half, rows_j, rank), out[:, rank:].reshape(half, rows_j, rank)], 0
    )


def place_kernel(axis, weight, *refs):
    *ins, out = refs
    rows = ins[0].shape[0]
    digit = digit_of(axis, weight, len(ins))
    for q, ref in enumerate(ins):
        out[pl.ds(pl.multiple_of((digit ^ q) * rows, rows), rows)] = ref[...]


def gather_digit(x, axis, weight, radix):
    got = [swap(x, axis, weight, q) for q in range(1, radix)]
    (x,) = call(
        functools.partial(place_kernel, axis, weight),
        [((x.shape[0] * radix, x.shape[1]), x.dtype)],
        x, *got,
        flops=PLACE_FLOPS,
    )
    return x


def gather(x, axis):
    for weight, radix in digits(lax.axis_size(axis)):
        x = gather_digit(x, axis, weight, radix)
    return x


def add_kernel(norm_at, *refs):
    *ins, out = refs
    out[...] = sum_rows(ins, 0, out.shape[0]).astype(BF16)
    if norm_at is not None:
        put_norm(out, norm_at, sum_norm(ins, norm_at))


def sum_parts(x, axis, norm_at=None):
    parts = [x]
    for weight, radix in digits(lax.axis_size(axis)):
        if len(parts) > 1:
            (x,) = call(functools.partial(add_kernel, norm_at), [(x.shape, BF16)], *parts)
        parts = [x] + [swap(x, axis, weight, q) for q in range(1, radix)]
    return parts


def sum_c(t_ref, a_ref, b16, acc):
    rows_i, rows_j, depth = t_ref.shape
    group = divisor(rows_i, 32)
    acc[...] = jnp.zeros_like(acc)

    def step(g, carry):
        at = pl.ds(pl.multiple_of(g * group, group), group)
        a16 = a_ref[at].astype(BF16)
        pairs = jnp.concatenate([a16[q : q + 1] * b16 for q in range(group)], 0)
        acc[...] += dot_rows(t_ref[at].reshape(group * rows_j, depth), pairs)
        return carry

    lax.fori_loop(0, rows_i // group, step, 0)


def first_kernel(t_ref, a_ref, b_ref, c_ref, row_ref, col_ref, acc_a, acc_b, acc_c):
    rows_i, rows_j, depth = t_ref.shape
    group = divisor(rows_i, 64)
    a16 = a_ref[...].astype(BF16)
    b16 = b_ref[...].astype(BF16)
    c16 = c_ref[...].astype(BF16)
    b32 = b16.astype(F32)
    pair_c = twice(c16)
    acc_b[...] = jnp.zeros_like(acc_b)
    acc_c[...] = jnp.zeros_like(acc_c)

    def step(g, carry):
        at = pl.ds(pl.multiple_of(g * group, group), group)
        part16 = a_ref[at].astype(BF16)
        part32 = part16.astype(F32)
        block = t_ref[at]
        along = times_c(block, pair_c)
        acc_a[at] = jnp.sum(along * b32[None], axis=1)
        total = acc_b[...]
        for q in range(group):
            total = total + along[q] * part32[q : q + 1]
        acc_b[...] = total
        pairs = jnp.concatenate([part16[q : q + 1] * b16 for q in range(group)], 0)
        acc_c[...] += dot_rows(block.reshape(group * rows_j, depth), pairs)
        return carry

    lax.fori_loop(0, rows_i // group, step, 0)
    gram_a, gram_b, gram_c = gram(a16), gram(b16), gram(c16)
    row_ref[:rows_j] = (acc_b[...] - dot_wide(b16, gram_a * gram_c)).astype(BF16)
    row_ref[rows_j : rows_j + depth] = (acc_c[...] - dot_wide(c16, gram_a * gram_b)).astype(BF16)
    put_norm(row_ref, rows_j + depth, squares(a16))
    col_ref[:rows_i] = (acc_a[...] - dot_wide(a16, gram_b * gram_c)).astype(BF16)
    put_norm(col_ref, rows_i, squares(b16))


def middle_kernel(n_row, n_col, *refs):
    rows, refs = refs[:n_row], refs[n_row:]
    cols, refs = refs[:n_col], refs[n_col:]
    a_ref, b_ref, c_ref, new_a, new_b, part_c, step_c = refs
    rows_i, rows_j, depth = a_ref.shape[0], b_ref.shape[0], c_ref.shape[0]
    norm_a = sum_norm(rows, rows_j + depth)
    norm_b = sum_norm(cols, rows_i)
    norm_c = squares(c_ref[...].astype(BF16))
    step_a = scaling / (norm_b * norm_c + epsilon)
    step_b = scaling / (norm_a * norm_c + epsilon)
    new_a[...] = damping * a_ref[...] + step_a * sum_rows(cols, 0, rows_i)
    new_b[...] = damping * b_ref[...] + step_b * sum_rows(rows, 0, rows_j)
    part_c[...] = sum_rows(rows, rows_j, depth).astype(BF16)
    step_c[...] = jnp.broadcast_to(scaling / (norm_a * norm_b + epsilon), step_c.shape)


def second_c_kernel(t_ref, a_ref, b_ref, sum_ref, gram_ref):
    a16 = a_ref[...].astype(BF16)
    b16 = b_ref[...].astype(BF16)
    sum_c(t_ref, a_ref, b16, sum_ref)
    gram_ref[...] = gram(a16) * gram(b16)


def second_model_kernel(n_col, *refs):
    parts, refs = refs[:n_col], refs[n_col:]
    step_ref, c_ref, sum_ref, gram_ref, new_c, out_ref = refs
    c2 = damping * c_ref[...] + step_ref[0:1] * sum_rows(parts, 0, c_ref.shape[0])
    new_c[...] = c2
    out_ref[...] = (sum_ref[...] - dot_wide(c2.astype(BF16), gram_ref[...])).astype(BF16)


def second_ab_kernel(t_ref, a_ref, b_ref, c_ref, col_ref, grad_b, acc_a):
    rows_i, rows_j, depth = t_ref.shape
    group = divisor(rows_i, 32)
    a16 = a_ref[...].astype(BF16)
    b16 = b_ref[...].astype(BF16)
    c16 = c_ref[...].astype(BF16)
    b32 = b16.astype(F32)
    pair_c = twice(c16)
    grad_b[...] = jnp.zeros_like(grad_b)

    def step(g, carry):
        at = pl.ds(pl.multiple_of(g * group, group), group)
        a32 = a_ref[at].astype(BF16).astype(F32)
        along = times_c(t_ref[at], pair_c)
        acc_a[at] = jnp.sum(along * b32[None], axis=1)
        total = grad_b[...]
        for q in range(group):
            total = total + along[q] * a32[q : q + 1]
        grad_b[...] = total
        return carry

    lax.fori_loop(0, rows_i // group, step, 0)
    gram_c = gram(c16)
    col_ref[:rows_i] = (acc_a[...] - dot_wide(a16, gram(b16) * gram_c)).astype(BF16)
    put_norm(col_ref, rows_i, squares(b16))
    grad_b[...] -= dot_wide(b16, gram(a16) * gram_c)


def put_shares(weight, own_j, shared, norm, grad_b, outs):
    radix = len(outs)
    depth = shared.shape[0]
    blocks = grad_b.shape[0] // own_j
    digit = digit_of("row", weight, radix)
    for q, out in enumerate(outs):
        out[:depth] = shared
        put_norm(out, depth, norm)
        first = [(high * radix + (digit ^ q)) * own_j for high in range(blocks // radix)]
        rows = [grad_b[pl.ds(pl.multiple_of(at, own_j), own_j)] for at in first]
        out[depth + NORM_ROWS :] = jnp.concatenate(rows, 0).astype(BF16)


def shares_kernel(n_col, own_j, radix, *refs):
    parts, refs = refs[:n_col], refs[n_col:]
    a_ref, grad_b, outs = refs[0], refs[1], refs[2:]
    shared = sum_rows(parts, 0, parts[0].shape[0]).astype(BF16)
    put_shares(1, own_j, shared, squares(a_ref[...].astype(BF16)), grad_b, outs)


def next_shares_kernel(n_row, weight, own_j, depth, *refs):
    parts, outs, grad_b = refs[:n_row], refs[n_row:-1], refs[-1]
    shared = sum_rows(parts, 0, depth).astype(BF16)
    grad_b[...] = sum_rows(parts, depth + NORM_ROWS, grad_b.shape[0])
    put_shares(weight, own_j, shared, sum_norm(parts, depth), grad_b, outs)


def sum_shares(col_parts, a, grad_b, own_j):
    depth, rank = col_parts[0].shape
    stages = list(digits(lax.axis_size("row")))
    held = grad_b.shape[0]
    parts = None
    for weight, radix in stages:
        shape = (depth + NORM_ROWS + held // radix, rank)
        outs = [(shape, BF16)] * radix
        if parts is None:
            sent = call(
                functools.partial(shares_kernel, len(col_parts), own_j, radix),
                outs, *col_parts, a, grad_b,
            )
        else:
            sent = call(
                functools.partial(next_shares_kernel, len(parts), weight, own_j, depth),
                outs, *parts,
                scratch=[pltpu.VMEM((held, rank), F32)],
            )
        held //= radix
        parts = [sent[0]] + [swap(sent[q], "row", weight, q) for q in range(1, radix)]
    return parts


def last_kernel(n_row, n_col, *refs):
    rows, refs = refs[:n_row], refs[n_row:]
    cols, refs = refs[:n_col], refs[n_col:]
    a_ref, b_ref, c_ref, out_a, out_b, out_c, grad_a = refs
    rows_i, depth = a_ref.shape[0], c_ref.shape[0]
    own_i, own_j = out_a.shape[0], out_b.shape[0]
    norm_a = sum_norm(rows, depth)
    norm_b = sum_norm(cols, rows_i)
    norm_c = squares(c_ref[...].astype(BF16))
    step_a = scaling / (norm_b * norm_c + epsilon)
    step_b = scaling / (norm_a * norm_c + epsilon)
    step_c = scaling / (norm_a * norm_b + epsilon)
    grad_a[...] = sum_rows(cols, 0, rows_i)
    at_i = pl.ds(pl.multiple_of(lax.axis_index("col") * own_i, own_i), own_i)
    at_j = pl.ds(pl.multiple_of(lax.axis_index("row") * own_j, own_j), own_j)
    out_a[...] = damping * a_ref[at_i] + step_a * grad_a[at_i]
    out_b[...] = damping * b_ref[at_j] + step_b * sum_rows(rows, depth + NORM_ROWS, own_j)
    out_c[...] = damping * c_ref[...] + step_c * sum_rows(rows, 0, depth)


def local(tensor, factor_a, factor_b, factor_c):
    rows_i, rows_j, depth = tensor.shape
    rank = factor_a.shape[1]
    own_j = factor_b.shape[0]
    c = factor_c
    b = gather(factor_b, "row")
    a = gather(factor_a, "col")

    to_row, to_col = call(
        first_kernel,
        [((rows_j + depth + NORM_ROWS, rank), BF16), ((rows_i + NORM_ROWS, rank), BF16)],
        tensor, a, b, c,
        scratch=[pltpu.VMEM((n, rank), F32) for n in (rows_i, rows_j, depth)],
        flops=6 * tensor.size * rank,
    )
    rows = sum_parts(to_row, "row", rows_j + depth)
    cols = sum_parts(to_col, "col", rows_i)
    a, b, part_c, step_c = call(
        functools.partial(middle_kernel, len(rows), len(cols)),
        [(a.shape, F32), (b.shape, F32), (c.shape, BF16), ((8, rank), F32)],
        *rows, *cols, a, b, c,
    )

    parts = sum_parts(part_c, "col")
    sum_t, gram_ab = call(
        second_c_kernel,
        [(c.shape, F32), ((rank, rank), F32)],
        tensor, a, b,
        flops=2 * tensor.size * rank,
    )
    c, to_col = call(
        functools.partial(second_model_kernel, len(parts)),
        [(c.shape, F32), (c.shape, BF16)],
        *parts, step_c, c, sum_t, gram_ab,
    )
    parts = sum_parts(to_col, "col")
    to_col, grad_b = call(
        second_ab_kernel,
        [((rows_i + NORM_ROWS, rank), BF16), ((rows_j, rank), F32)],
        tensor, a, b, c,
        scratch=[pltpu.VMEM((rows_i, rank), F32)],
        flops=2 * tensor.size * rank,
    )
    rows = sum_shares(parts, a, grad_b, own_j)
    cols = sum_parts(to_col, "col", rows_i)
    return call(
        functools.partial(last_kernel, len(rows), len(cols)),
        [(factor_a.shape, F32), (factor_b.shape, F32), (c.shape, F32)],
        *rows, *cols, a, b, c,
        scratch=[pltpu.VMEM((rows_i, rank), F32)],
        hbm_out=True,
    )


def solution(mesh):
    return jax.shard_map(
        local,
        mesh=mesh,
        in_specs=(P("row", "col", None), P(("row", "col"), None), P(("col", "row"), None), P()),
        out_specs=(P(("row", "col"), None), P(("col", "row"), None), P()),
        check_vma=False,
    )
```

```python
import functools

import jax
import jax.numpy as jnp
from jax import lax
from jax.experimental import pallas as pl
from jax.experimental.pallas import tpu as pltpu
from jax.sharding import PartitionSpec as P

F32 = jnp.float32
BF16 = jnp.bfloat16
NORM_ROWS = 16
VMEM_LIMIT = 24 << 20
HOLD_FLOPS = 5 * 10**9
PLACE_FLOPS = 2 * 10**9


damping = 0.9
scaling = 0.25
epsilon = 1e-06


def vmem(x):
    return pltpu.with_memory_space_constraint(x, pltpu.VMEM)


def call(body, outs, *operands, scratch=(), hbm_out=False, flops=0):
    whole = pl.BlockSpec(memory_space=pltpu.VMEM)
    place = jax.ShapeDtypeStruct if hbm_out else pltpu.VMEM
    return pl.pallas_call(
        body,
        in_specs=[whole] * len(operands),
        out_specs=[whole] * len(outs),
        out_shape=[place(s, d) for s, d in outs],
        scratch_shapes=scratch,
        cost_estimate=pl.CostEstimate(flops=flops, bytes_accessed=0, transcendentals=0),
        compiler_params=pltpu.CompilerParams(vmem_limit_bytes=VMEM_LIMIT),
    )(*[vmem(x) for x in operands])


def divisor(n, most):
    return next(g for g in (256, 128, 64, 32, 16, 8, 4, 2) if g <= most and n % g == 0)


def dot(x, y):
    return jnp.dot(x, y, preferred_element_type=F32)


def dot_rows(x, y):
    return lax.dot_general(x, y, (((0,), (0,)), ((), ())), preferred_element_type=F32)


def gram(x16):
    return dot_rows(x16, x16)


def dot_wide(x16, y):
    high = y.astype(BF16)
    low = (y - high.astype(F32)).astype(BF16)
    return dot(x16, high) + dot(x16, low)


def put_norm(ref, start, norm):
    high = norm.astype(BF16).astype(F32)
    rest = norm - high
    mid = rest.astype(BF16).astype(F32)
    low = rest - mid
    rows = jnp.concatenate([high, mid, low, jnp.zeros((NORM_ROWS - 3, norm.shape[1]), F32)], 0)
    ref[start : start + NORM_ROWS] = rows.astype(BF16)


def get_norm(ref, start):
    rows = ref[start : start + NORM_ROWS].astype(F32)
    return rows[0:1] + rows[1:2] + rows[2:3]


def squares(x16):
    return jnp.sum(jnp.square(x16.astype(F32)), axis=0, keepdims=True)


def tree(parts):
    while len(parts) > 1:
        parts = [parts[q] + parts[q + 1] for q in range(0, len(parts), 2)]
    return parts[0]


def sum_rows(refs, start, rows):
    return tree([r[start : start + rows].astype(F32) for r in refs])


def sum_norm(refs, start):
    return tree([get_norm(r, start) for r in refs])


def digits(n):
    weight = 1
    while weight < n:
        radix = 4 if (n // weight) % 4 == 0 else 2
        yield weight, radix
        weight *= radix


def digit_of(axis, weight, radix):
    return lax.rem(lax.div(lax.axis_index(axis), weight), radix)


def swap(x, axis, weight, q):
    return lax.ppermute(x, axis, [(i, i ^ (q * weight)) for i in range(lax.axis_size(axis))])


def twice(c16):
    zero = jnp.zeros_like(c16)
    return jnp.concatenate(
        [jnp.concatenate([c16, zero], 1), jnp.concatenate([zero, c16], 1)], 0
    )


def place_kernel(axis, weight, *refs):
    *ins, out = refs
    rows = ins[0].shape[0]
    digit = digit_of(axis, weight, len(ins))
    for q, ref in enumerate(ins):
        out[pl.ds(pl.multiple_of((digit ^ q) * rows, rows), rows)] = ref[...]


def gather_digit(x, own, axis, weight, radix):
    got = [swap(x, axis, weight, q) for q in range(1, radix)]
    (x,) = call(
        functools.partial(place_kernel, axis, weight),
        [((x.shape[0] * radix, x.shape[1]), x.dtype)],
        own, *got,
        flops=PLACE_FLOPS,
    )
    return x


def gather(x, own, axis):
    for weight, radix in digits(lax.axis_size(axis)):
        x = own = gather_digit(x, own, axis, weight, radix)
    return x


def hold_kernel(*refs):
    half = len(refs) // 2
    for ref, out in zip(refs[:half], refs[half:]):
        out[...] = ref[...]


def hold(*arrays):
    whole = pl.BlockSpec(memory_space=pltpu.VMEM)
    return pl.pallas_call(
        hold_kernel,
        out_specs=[whole] * len(arrays),
        out_shape=[pltpu.VMEM(x.shape, x.dtype) for x in arrays],
        cost_estimate=pl.CostEstimate(flops=HOLD_FLOPS, bytes_accessed=0, transcendentals=0),
    )(*[pltpu.with_memory_space_constraint(x, pltpu.HBM) for x in arrays])


def add_kernel(norm_at, *refs):
    *ins, out = refs
    out[...] = sum_rows(ins, 0, out.shape[0]).astype(BF16)
    if norm_at is not None:
        put_norm(out, norm_at, sum_norm(ins, norm_at))


def sum_parts(x, axis, norm_at=None):
    parts = [x]
    for weight, radix in digits(lax.axis_size(axis)):
        if len(parts) > 1:
            (x,) = call(functools.partial(add_kernel, norm_at), [(x.shape, BF16)], *parts)
        parts = [x] + [swap(x, axis, weight, q) for q in range(1, radix)]
    return parts


def sum_c(t_ref, a_ref, b16, acc):
    rows_i, rows_j, depth = t_ref.shape
    group = divisor(rows_i, 256)
    acc[...] = jnp.zeros_like(acc)

    def step(g, carry):
        at = pl.ds(pl.multiple_of(g * group, group), group)
        a16 = a_ref[at].astype(BF16)
        pairs = jnp.concatenate([a16[q : q + 1] * b16 for q in range(group)], 0)
        acc[...] += dot_rows(t_ref[at].reshape(group * rows_j, depth), pairs)
        return carry

    lax.fori_loop(0, rows_i // group, step, 0)


def sum_b(t_ref, a_ref, c16, acc):
    rows_i, rows_j, depth = t_ref.shape
    group = divisor(rows_i, 256)
    acc[...] = jnp.zeros_like(acc)

    def step(g, carry):
        at = pl.ds(pl.multiple_of(g * group, group), group)
        a16 = a_ref[at].astype(BF16)
        pairs = jnp.concatenate([a16[q : q + 1] * c16 for q in range(group)], 0)
        block = t_ref[at]
        acc[...] += dot(jnp.concatenate([block[q] for q in range(group)], 1), pairs)
        return carry

    lax.fori_loop(0, rows_i // group, step, 0)


def sum_a(t_ref, a_ref, b16, c16, acc, acc_b=None):
    rows_i, rows_j, depth = t_ref.shape
    rank = c16.shape[1]
    group = divisor(rows_i, 256)
    half = group // 2
    b32 = b16.astype(F32)
    pair_c = twice(c16)
    if acc_b is not None:
        acc_b[...] = jnp.zeros_like(acc_b)

    def step(g, carry):
        at = pl.ds(pl.multiple_of(g * group, group), group)
        block = t_ref[at]
        if acc_b is not None:
            a32 = a_ref[at].astype(BF16).astype(F32)
            total = acc_b[...]
        sums = [None] * group
        for q in range(half):
            along = dot(jnp.concatenate([block[q], block[q + half]], 1), pair_c)
            for i, part in ((q, along[:, :rank]), (q + half, along[:, rank:])):
                sums[i] = jnp.sum(part * b32, axis=0, keepdims=True)
                if acc_b is not None:
                    total = total + part * a32[i : i + 1]
        acc[at] = jnp.concatenate(sums, 0)
        if acc_b is not None:
            acc_b[...] = total
        return carry

    lax.fori_loop(0, rows_i // group, step, 0)


def first_b_kernel(t_ref, a_ref, c_ref, acc):
    sum_b(t_ref, a_ref, c_ref[...].astype(BF16), acc)


def first_c_kernel(t_ref, a_ref, b_ref, c_ref, acc_b, row_ref, acc_c):
    rows_j, depth = b_ref.shape[0], c_ref.shape[0]
    a16 = a_ref[...].astype(BF16)
    b16 = b_ref[...].astype(BF16)
    c16 = c_ref[...].astype(BF16)
    sum_c(t_ref, a_ref, b16, acc_c)
    gram_a, gram_b, gram_c = gram(a16), gram(b16), gram(c16)
    row_ref[:rows_j] = (acc_b[...] - dot_wide(b16, gram_a * gram_c)).astype(BF16)
    row_ref[rows_j : rows_j + depth] = (acc_c[...] - dot_wide(c16, gram_a * gram_b)).astype(BF16)
    put_norm(row_ref, rows_j + depth, squares(a16))


def first_a_kernel(t_ref, a_ref, b_ref, c_ref, col_ref, acc_a):
    rows_i = a_ref.shape[0]
    a16 = a_ref[...].astype(BF16)
    b16 = b_ref[...].astype(BF16)
    c16 = c_ref[...].astype(BF16)
    sum_a(t_ref, a_ref, b16, c16, acc_a)
    col_ref[:rows_i] = (acc_a[...] - dot_wide(a16, gram(b16) * gram(c16))).astype(BF16)
    put_norm(col_ref, rows_i, squares(b16))


def middle_kernel(n_row, n_col, *refs):
    rows, refs = refs[:n_row], refs[n_row:]
    cols, refs = refs[:n_col], refs[n_col:]
    a_ref, b_ref, c_ref, new_a, new_b, part_c, step_c = refs
    rows_i, rows_j, depth = a_ref.shape[0], b_ref.shape[0], c_ref.shape[0]
    norm_a = sum_norm(rows, rows_j + depth)
    norm_b = sum_norm(cols, rows_i)
    norm_c = squares(c_ref[...].astype(BF16))
    step_a = scaling / (norm_b * norm_c + epsilon)
    step_b = scaling / (norm_a * norm_c + epsilon)
    new_a[...] = damping * a_ref[...] + step_a * sum_rows(cols, 0, rows_i)
    new_b[...] = damping * b_ref[...] + step_b * sum_rows(rows, 0, rows_j)
    part_c[...] = sum_rows(rows, rows_j, depth).astype(BF16)
    step_c[...] = jnp.broadcast_to(scaling / (norm_a * norm_b + epsilon), step_c.shape)


def second_c_kernel(t_ref, a_ref, b_ref, sum_ref, gram_ref):
    a16 = a_ref[...].astype(BF16)
    b16 = b_ref[...].astype(BF16)
    sum_c(t_ref, a_ref, b16, sum_ref)
    gram_ref[...] = gram(a16) * gram(b16)


def second_model_kernel(n_col, *refs):
    parts, refs = refs[:n_col], refs[n_col:]
    step_ref, c_ref, sum_ref, gram_ref, new_c, out_ref = refs
    c2 = damping * c_ref[...] + step_ref[0:1] * sum_rows(parts, 0, c_ref.shape[0])
    new_c[...] = c2
    out_ref[...] = (sum_ref[...] - dot_wide(c2.astype(BF16), gram_ref[...])).astype(BF16)


def second_ab_kernel(t_ref, a_ref, b_ref, c_ref, col_ref, grad_b, acc_a):
    rows_i = a_ref.shape[0]
    a16 = a_ref[...].astype(BF16)
    b16 = b_ref[...].astype(BF16)
    c16 = c_ref[...].astype(BF16)
    sum_a(t_ref, a_ref, b16, c16, acc_a, grad_b)
    gram_c = gram(c16)
    col_ref[:rows_i] = (acc_a[...] - dot_wide(a16, gram(b16) * gram_c)).astype(BF16)
    put_norm(col_ref, rows_i, squares(b16))
    grad_b[...] -= dot_wide(b16, gram(a16) * gram_c)


def put_shares(weight, own_j, shared, norm, grad_b, outs):
    radix = len(outs)
    depth = shared.shape[0]
    blocks = grad_b.shape[0] // own_j
    digit = digit_of("row", weight, radix)
    for q, out in enumerate(outs):
        out[:depth] = shared
        put_norm(out, depth, norm)
        first = [(high * radix + (digit ^ q)) * own_j for high in range(blocks // radix)]
        rows = [grad_b[pl.ds(pl.multiple_of(at, own_j), own_j)] for at in first]
        out[depth + NORM_ROWS :] = jnp.concatenate(rows, 0).astype(BF16)


def shares_kernel(n_col, own_j, radix, *refs):
    parts, refs = refs[:n_col], refs[n_col:]
    a_ref, grad_b, outs = refs[0], refs[1], refs[2:]
    shared = sum_rows(parts, 0, parts[0].shape[0]).astype(BF16)
    put_shares(1, own_j, shared, squares(a_ref[...].astype(BF16)), grad_b, outs)


def next_shares_kernel(n_row, weight, own_j, depth, *refs):
    parts, outs, grad_b = refs[:n_row], refs[n_row:-1], refs[-1]
    shared = sum_rows(parts, 0, depth).astype(BF16)
    grad_b[...] = sum_rows(parts, depth + NORM_ROWS, grad_b.shape[0])
    put_shares(weight, own_j, shared, sum_norm(parts, depth), grad_b, outs)


def sum_shares(col_parts, a, grad_b, own_j):
    depth, rank = col_parts[0].shape
    stages = list(digits(lax.axis_size("row")))
    held = grad_b.shape[0]
    parts = None
    for weight, radix in stages:
        shape = (depth + NORM_ROWS + held // radix, rank)
        outs = [(shape, BF16)] * radix
        if parts is None:
            sent = call(
                functools.partial(shares_kernel, len(col_parts), own_j, radix),
                outs, *col_parts, a, grad_b,
            )
        else:
            sent = call(
                functools.partial(next_shares_kernel, len(parts), weight, own_j, depth),
                outs, *parts,
                scratch=[pltpu.VMEM((held, rank), F32)],
            )
        held //= radix
        parts = [sent[0]] + [swap(sent[q], "row", weight, q) for q in range(1, radix)]
    return parts


def last_kernel(n_row, n_col, *refs):
    rows, refs = refs[:n_row], refs[n_row:]
    cols, refs = refs[:n_col], refs[n_col:]
    a_ref, b_ref, c_ref, out_a, out_b, out_c, grad_a = refs
    rows_i, depth = a_ref.shape[0], c_ref.shape[0]
    own_i, own_j = out_a.shape[0], out_b.shape[0]
    norm_a = sum_norm(rows, depth)
    norm_b = sum_norm(cols, rows_i)
    norm_c = squares(c_ref[...].astype(BF16))
    step_a = scaling / (norm_b * norm_c + epsilon)
    step_b = scaling / (norm_a * norm_c + epsilon)
    step_c = scaling / (norm_a * norm_b + epsilon)
    grad_a[...] = sum_rows(cols, 0, rows_i)
    at_i = pl.ds(pl.multiple_of(lax.axis_index("col") * own_i, own_i), own_i)
    at_j = pl.ds(pl.multiple_of(lax.axis_index("row") * own_j, own_j), own_j)
    out_a[...] = damping * a_ref[at_i] + step_a * grad_a[at_i]
    out_b[...] = damping * b_ref[at_j] + step_b * sum_rows(rows, depth + NORM_ROWS, own_j)
    out_c[...] = damping * c_ref[...] + step_c * sum_rows(rows, 0, depth)


def local(tensor, factor_a, factor_b, factor_c):
    rows_i, rows_j, depth = tensor.shape
    rank = factor_a.shape[1]
    own_j = factor_b.shape[0]
    held_a, held_b, c = hold(factor_a, factor_b, factor_c)
    b = gather(factor_b, held_b, "row")
    a = gather(factor_a, held_a, "col")

    (grad_b,) = call(
        first_b_kernel, [(b.shape, F32)], tensor, a, c, flops=2 * tensor.size * rank
    )
    (to_row,) = call(
        first_c_kernel,
        [((rows_j + depth + NORM_ROWS, rank), BF16)],
        tensor, a, b, c, grad_b,
        scratch=[pltpu.VMEM(c.shape, F32)],
        flops=2 * tensor.size * rank,
    )
    (to_col,) = call(
        first_a_kernel,
        [((rows_i + NORM_ROWS, rank), BF16)],
        tensor, a, b, c,
        scratch=[pltpu.VMEM(a.shape, F32)],
        flops=2 * tensor.size * rank,
    )
    rows = sum_parts(to_row, "row", rows_j + depth)
    cols = sum_parts(to_col, "col", rows_i)
    a, b, part_c, step_c = call(
        functools.partial(middle_kernel, len(rows), len(cols)),
        [(a.shape, F32), (b.shape, F32), (c.shape, BF16), ((8, rank), F32)],
        *rows, *cols, a, b, c,
    )

    parts = sum_parts(part_c, "col")
    sum_t, gram_ab = call(
        second_c_kernel,
        [(c.shape, F32), ((rank, rank), F32)],
        tensor, a, b,
        flops=2 * tensor.size * rank,
    )
    c, to_col = call(
        functools.partial(second_model_kernel, len(parts)),
        [(c.shape, F32), (c.shape, BF16)],
        *parts, step_c, c, sum_t, gram_ab,
    )
    parts = sum_parts(to_col, "col")
    to_col, grad_b = call(
        second_ab_kernel,
        [((rows_i + NORM_ROWS, rank), BF16), ((rows_j, rank), F32)],
        tensor, a, b, c,
        scratch=[pltpu.VMEM((rows_i, rank), F32)],
        flops=2 * tensor.size * rank,
    )
    rows = sum_shares(parts, a, grad_b, own_j)
    cols = sum_parts(to_col, "col", rows_i)
    return call(
        functools.partial(last_kernel, len(rows), len(cols)),
        [(factor_a.shape, F32), (factor_b.shape, F32), (c.shape, F32)],
        *rows, *cols, a, b, c,
        scratch=[pltpu.VMEM((rows_i, rank), F32)],
        hbm_out=True,
    )


def solution(mesh):
    return jax.shard_map(
        local,
        mesh=mesh,
        in_specs=(P("row", "col", None), P(("row", "col"), None), P(("col", "row"), None), P()),
        out_specs=(P(("row", "col"), None), P(("col", "row"), None), P()),
        check_vma=False,
    )
```

```python
import functools

import jax
import jax.numpy as jnp
from jax import lax
from jax.experimental import pallas as pl
from jax.experimental.pallas import tpu as pltpu
from jax.sharding import PartitionSpec as P

F32 = jnp.float32
BF16 = jnp.bfloat16
NORM_ROWS = 16
VMEM_LIMIT = 24 << 20
HOLD_FLOPS = 5 * 10**9
PLACE_FLOPS = 2 * 10**9


damping = 0.9
scaling = 0.25
epsilon = 1e-06


def vmem(x):
    return pltpu.with_memory_space_constraint(x, pltpu.VMEM)


def call(body, outs, *operands, scratch=(), hbm_out=False, flops=0):
    whole = pl.BlockSpec(memory_space=pltpu.VMEM)
    place = jax.ShapeDtypeStruct if hbm_out else pltpu.VMEM
    return pl.pallas_call(
        body,
        in_specs=[whole] * len(operands),
        out_specs=[whole] * len(outs),
        out_shape=[place(s, d) for s, d in outs],
        scratch_shapes=scratch,
        cost_estimate=pl.CostEstimate(flops=flops, bytes_accessed=0, transcendentals=0),
        compiler_params=pltpu.CompilerParams(vmem_limit_bytes=VMEM_LIMIT),
    )(*[vmem(x) for x in operands])


def divisor(n, most):
    return next(g for g in (256, 128, 64, 32, 16, 8, 4, 2) if g <= most and n % g == 0)


def dot(x, y):
    return jnp.dot(x, y, preferred_element_type=F32)


def dot_rows(x, y):
    return lax.dot_general(x, y, (((0,), (0,)), ((), ())), preferred_element_type=F32)


def gram(x16):
    return dot_rows(x16, x16)


def dot_wide(x16, y):
    high = y.astype(BF16)
    low = (y - high.astype(F32)).astype(BF16)
    return dot(x16, high) + dot(x16, low)


def put_norm(ref, start, norm):
    high = norm.astype(BF16).astype(F32)
    rest = norm - high
    mid = rest.astype(BF16).astype(F32)
    low = rest - mid
    rows = jnp.concatenate([high, mid, low, jnp.zeros((NORM_ROWS - 3, norm.shape[1]), F32)], 0)
    ref[start : start + NORM_ROWS] = rows.astype(BF16)


def get_norm(ref, start):
    rows = ref[start : start + NORM_ROWS].astype(F32)
    return rows[0:1] + rows[1:2] + rows[2:3]


def squares(x16):
    return jnp.sum(jnp.square(x16.astype(F32)), axis=0, keepdims=True)


def tree(parts):
    while len(parts) > 1:
        parts = [parts[q] + parts[q + 1] for q in range(0, len(parts), 2)]
    return parts[0]


def sum_rows(refs, start, rows):
    return tree([r[start : start + rows].astype(F32) for r in refs])


def sum_norm(refs, start):
    return tree([get_norm(r, start) for r in refs])


def digits(n, most=4):
    weight = 1
    while weight < n:
        radix = 4 if most == 4 and (n // weight) % 4 == 0 else 2
        yield weight, radix
        weight *= radix


def digit_of(axis, weight, radix):
    return lax.rem(lax.div(lax.axis_index(axis), weight), radix)


def swap(x, axis, weight, q):
    return lax.ppermute(x, axis, [(i, i ^ (q * weight)) for i in range(lax.axis_size(axis))])


def turns(radix):
    return [0] + list(range(radix - 1, 0, -1))


def twice(c16):
    zero = jnp.zeros_like(c16)
    return jnp.concatenate(
        [jnp.concatenate([c16, zero], 1), jnp.concatenate([zero, c16], 1)], 0
    )


def place_kernel(axis, weight, *refs):
    *ins, out = refs
    rows = ins[0].shape[0]
    digit = digit_of(axis, weight, len(ins))
    for q, ref in zip(turns(len(ins)), ins):
        out[pl.ds(pl.multiple_of((digit ^ q) * rows, rows), rows)] = ref[...]


def gather_digit(x, own, axis, weight, radix):
    got = [swap(x, axis, weight, q) for q in turns(radix)[1:]]
    (x,) = call(
        functools.partial(place_kernel, axis, weight),
        [((x.shape[0] * radix, x.shape[1]), x.dtype)],
        own, *got,
        flops=PLACE_FLOPS,
    )
    return x


def gather(x, own, axis):
    for weight, radix in digits(lax.axis_size(axis)):
        x = own = gather_digit(x, own, axis, weight, radix)
    return x


def hold_kernel(*refs):
    half = len(refs) // 2
    for ref, out in zip(refs[:half], refs[half:]):
        out[...] = ref[...]


def hold(*arrays):
    whole = pl.BlockSpec(memory_space=pltpu.VMEM)
    return pl.pallas_call(
        hold_kernel,
        out_specs=[whole] * len(arrays),
        out_shape=[pltpu.VMEM(x.shape, x.dtype) for x in arrays],
        cost_estimate=pl.CostEstimate(flops=HOLD_FLOPS, bytes_accessed=0, transcendentals=0),
    )(*[pltpu.with_memory_space_constraint(x, pltpu.HBM) for x in arrays])


def add_kernel(norm_at, *refs):
    *ins, out = refs
    out[...] = sum_rows(ins, 0, out.shape[0]).astype(BF16)
    if norm_at is not None:
        put_norm(out, norm_at, sum_norm(ins, norm_at))


def sum_parts(x, axis, norm_at=None, most=4, high_first=False):
    parts = [x]
    order = list(digits(lax.axis_size(axis), most))
    for weight, radix in reversed(order) if high_first else order:
        if len(parts) > 1:
            (x,) = call(functools.partial(add_kernel, norm_at), [(x.shape, BF16)], *parts)
        parts = [x] + [swap(x, axis, weight, q) for q in range(1, radix)]
    return parts


def sum_c(t_ref, a_ref, b16, acc):
    rows_i, rows_j, depth = t_ref.shape
    group = divisor(rows_i, 256)
    acc[...] = jnp.zeros_like(acc)

    def step(g, carry):
        at = pl.ds(pl.multiple_of(g * group, group), group)
        a16 = a_ref[at].astype(BF16)
        pairs = jnp.concatenate([a16[q : q + 1] * b16 for q in range(group)], 0)
        acc[...] += dot_rows(t_ref[at].reshape(group * rows_j, depth), pairs)
        return carry

    lax.fori_loop(0, rows_i // group, step, 0)


def sum_b(t_ref, a_ref, c16, acc):
    rows_i, rows_j, depth = t_ref.shape
    group = divisor(rows_i, 256)
    acc[...] = jnp.zeros_like(acc)

    def step(g, carry):
        at = pl.ds(pl.multiple_of(g * group, group), group)
        a16 = a_ref[at].astype(BF16)
        pairs = jnp.concatenate([a16[q : q + 1] * c16 for q in range(group)], 0)
        block = t_ref[at]
        acc[...] += dot(jnp.concatenate([block[q] for q in range(group)], 1), pairs)
        return carry

    lax.fori_loop(0, rows_i // group, step, 0)


def sum_a(t_ref, a_ref, b16, c16, acc, acc_b=None):
    rows_i, rows_j, depth = t_ref.shape
    rank = c16.shape[1]
    group = divisor(rows_i, 256)
    half = group // 2
    b32 = b16.astype(F32)
    pair_c = twice(c16)
    if acc_b is not None:
        acc_b[...] = jnp.zeros_like(acc_b)

    def step(g, carry):
        at = pl.ds(pl.multiple_of(g * group, group), group)
        block = t_ref[at]
        if acc_b is not None:
            a32 = a_ref[at].astype(BF16).astype(F32)
            total = acc_b[...]
        sums = [None] * group
        for q in range(half):
            along = dot(jnp.concatenate([block[q], block[q + half]], 1), pair_c)
            for i, part in ((q, along[:, :rank]), (q + half, along[:, rank:])):
                sums[i] = jnp.sum(part * b32, axis=0, keepdims=True)
                if acc_b is not None:
                    total = total + part * a32[i : i + 1]
        acc[at] = jnp.concatenate(sums, 0)
        if acc_b is not None:
            acc_b[...] = total
        return carry

    lax.fori_loop(0, rows_i // group, step, 0)


def first_b_kernel(t_ref, a_ref, c_ref, acc):
    sum_b(t_ref, a_ref, c_ref[...].astype(BF16), acc)


def first_c_kernel(t_ref, a_ref, b_ref, c_ref, acc_b, row_ref, acc_c):
    rows_j, depth = b_ref.shape[0], c_ref.shape[0]
    a16 = a_ref[...].astype(BF16)
    b16 = b_ref[...].astype(BF16)
    c16 = c_ref[...].astype(BF16)
    sum_c(t_ref, a_ref, b16, acc_c)
    gram_a, gram_b, gram_c = gram(a16), gram(b16), gram(c16)
    row_ref[:rows_j] = (acc_b[...] - dot_wide(b16, gram_a * gram_c)).astype(BF16)
    row_ref[rows_j : rows_j + depth] = (acc_c[...] - dot_wide(c16, gram_a * gram_b)).astype(BF16)
    put_norm(row_ref, rows_j + depth, squares(a16))


def first_a_kernel(t_ref, a_ref, b_ref, c_ref, col_ref, acc_a):
    rows_i = a_ref.shape[0]
    a16 = a_ref[...].astype(BF16)
    b16 = b_ref[...].astype(BF16)
    c16 = c_ref[...].astype(BF16)
    sum_a(t_ref, a_ref, b16, c16, acc_a)
    col_ref[:rows_i] = (acc_a[...] - dot_wide(a16, gram(b16) * gram(c16))).astype(BF16)
    put_norm(col_ref, rows_i, squares(b16))


def middle_kernel(n_row, n_col, *refs):
    rows, refs = refs[:n_row], refs[n_row:]
    cols, refs = refs[:n_col], refs[n_col:]
    a_ref, b_ref, c_ref, new_a, new_b, part_c, step_c = refs
    rows_i, rows_j, depth = a_ref.shape[0], b_ref.shape[0], c_ref.shape[0]
    norm_a = sum_norm(rows, rows_j + depth)
    norm_b = sum_norm(cols, rows_i)
    norm_c = squares(c_ref[...].astype(BF16))
    step_a = scaling / (norm_b * norm_c + epsilon)
    step_b = scaling / (norm_a * norm_c + epsilon)
    new_a[...] = damping * a_ref[...] + step_a * sum_rows(cols, 0, rows_i)
    new_b[...] = damping * b_ref[...] + step_b * sum_rows(rows, 0, rows_j)
    part_c[...] = sum_rows(rows, rows_j, depth).astype(BF16)
    step_c[...] = jnp.broadcast_to(scaling / (norm_a * norm_b + epsilon), step_c.shape)


def second_c_kernel(t_ref, a_ref, b_ref, sum_ref, gram_ref):
    a16 = a_ref[...].astype(BF16)
    b16 = b_ref[...].astype(BF16)
    sum_c(t_ref, a_ref, b16, sum_ref)
    gram_ref[...] = gram(a16) * gram(b16)


def second_model_kernel(n_col, *refs):
    parts, refs = refs[:n_col], refs[n_col:]
    step_ref, c_ref, sum_ref, gram_ref, new_c, out_ref = refs
    c2 = damping * c_ref[...] + step_ref[0:1] * sum_rows(parts, 0, c_ref.shape[0])
    new_c[...] = c2
    out_ref[...] = (sum_ref[...] - dot_wide(c2.astype(BF16), gram_ref[...])).astype(BF16)


def second_b_kernel(t_ref, a_ref, b_ref, c_ref, grad_b):
    a16 = a_ref[...].astype(BF16)
    c16 = c_ref[...].astype(BF16)
    sum_b(t_ref, a_ref, c16, grad_b)
    grad_b[...] -= dot_wide(b_ref[...].astype(BF16), gram(a16) * gram(c16))


def second_a_kernel(weight, own_i, t_ref, a_ref, b_ref, c_ref, *refs):
    *outs, acc_a = refs
    b16 = b_ref[...].astype(BF16)
    c16 = c_ref[...].astype(BF16)
    sum_a(t_ref, a_ref, b16, c16, acc_a)
    acc_a[...] -= dot_wide(a_ref[...].astype(BF16), gram(b16) * gram(c16))
    put_shares("col", weight, own_i, None, squares(b16), acc_a, outs)


def put_shares(axis, weight, own, shared, norm, grad, outs):
    radix = len(outs)
    depth = 0 if shared is None else shared.shape[0]
    blocks = grad.shape[0] // own
    digit = digit_of(axis, weight, radix)
    for q, out in zip(turns(radix), outs):
        if depth:
            out[:depth] = shared
        put_norm(out, depth, norm)
        first = [(high * radix + (digit ^ q)) * own for high in range(blocks // radix)]
        rows = [grad[pl.ds(pl.multiple_of(at, own), own)] for at in first]
        out[depth + NORM_ROWS :] = jnp.concatenate(rows, 0).astype(BF16)


def shares_kernel(n_col, own_j, weight, *refs):
    parts, refs = refs[:n_col], refs[n_col:]
    a_ref, grad_b, outs = refs[0], refs[1], refs[2:]
    shared = sum_rows(parts, 0, parts[0].shape[0]).astype(BF16)
    put_shares("row", weight, own_j, shared, squares(a_ref[...].astype(BF16)), grad_b, outs)


def next_shares_kernel(axis, weight, own, depth, n_parts, *refs):
    parts, outs, grad = refs[:n_parts], refs[n_parts:-1], refs[-1]
    shared = sum_rows(parts, 0, depth).astype(BF16) if depth else None
    grad[...] = sum_rows(parts, depth + NORM_ROWS, grad.shape[0])
    put_shares(axis, weight, own, shared, sum_norm(parts, depth), grad, outs)


def first_digit(axis):
    return next(digits(lax.axis_size(axis)))


def messages(depth, rows, rank, radix):
    return [((depth + NORM_ROWS + rows // radix, rank), BF16)] * radix


def sum_shares(sent, axis, own, depth, beside=None):
    rank = sent[0].shape[1]
    parts = None
    for weight, radix in digits(lax.axis_size(axis)):
        if parts is not None:
            held = parts[0].shape[0] - depth - NORM_ROWS
            sent = call(
                functools.partial(next_shares_kernel, axis, weight, own, depth, len(parts)),
                messages(depth, held, rank, radix),
                *parts,
                scratch=[pltpu.VMEM((held, rank), F32)],
            )
            if beside is not None:
                sent, beside = lax.optimization_barrier((sent, beside))
        got = [swap(x, axis, weight, q) for q, x in zip(turns(radix)[1:], sent[1:])]
        parts = [sent[0]] + got
    return parts if beside is None else (parts, beside)


def last_kernel(n_row, n_col, *refs):
    rows, refs = refs[:n_row], refs[n_row:]
    cols, refs = refs[:n_col], refs[n_col:]
    a_ref, b_ref, c_ref, out_a, out_b, out_c = refs
    depth = c_ref.shape[0]
    own_i, own_j = out_a.shape[0], out_b.shape[0]
    norm_a = sum_norm(rows, depth)
    norm_b = sum_norm(cols, 0)
    norm_c = squares(c_ref[...].astype(BF16))
    step_a = scaling / (norm_b * norm_c + epsilon)
    step_b = scaling / (norm_a * norm_c + epsilon)
    step_c = scaling / (norm_a * norm_b + epsilon)
    at_i = pl.ds(pl.multiple_of(lax.axis_index("col") * own_i, own_i), own_i)
    at_j = pl.ds(pl.multiple_of(lax.axis_index("row") * own_j, own_j), own_j)
    out_a[...] = damping * a_ref[at_i] + step_a * sum_rows(cols, NORM_ROWS, own_i)
    out_b[...] = damping * b_ref[at_j] + step_b * sum_rows(rows, depth + NORM_ROWS, own_j)
    out_c[...] = damping * c_ref[...] + step_c * sum_rows(rows, 0, depth)


def local(tensor, factor_a, factor_b, factor_c):
    rows_i, rows_j, depth = tensor.shape
    rank = factor_a.shape[1]
    held_a, held_b, c = hold(factor_a, factor_b, factor_c)
    b = gather(factor_b, held_b, "row")
    a = gather(factor_a, held_a, "col")

    (grad_b,) = call(
        first_b_kernel, [(b.shape, F32)], tensor, a, c, flops=2 * tensor.size * rank
    )
    (to_row,) = call(
        first_c_kernel,
        [((rows_j + depth + NORM_ROWS, rank), BF16)],
        tensor, a, b, c, grad_b,
        scratch=[pltpu.VMEM(c.shape, F32)],
        flops=2 * tensor.size * rank,
    )
    (to_col,) = call(
        first_a_kernel,
        [((rows_i + NORM_ROWS, rank), BF16)],
        tensor, a, b, c,
        scratch=[pltpu.VMEM(a.shape, F32)],
        flops=2 * tensor.size * rank,
    )
    rows = sum_parts(to_row, "row", rows_j + depth, high_first=True)
    cols = sum_parts(to_col, "col", rows_i)
    a, b, part_c, step_c = call(
        functools.partial(middle_kernel, len(rows), len(cols)),
        [(a.shape, F32), (b.shape, F32), (c.shape, BF16), ((8, rank), F32)],
        *rows, *cols, a, b, c,
    )

    parts = sum_parts(part_c, "col")
    sum_t, gram_ab = call(
        second_c_kernel,
        [(c.shape, F32), ((rank, rank), F32)],
        tensor, a, b,
        flops=2 * tensor.size * rank,
    )
    c, to_col = call(
        functools.partial(second_model_kernel, len(parts)),
        [(c.shape, F32), (c.shape, BF16)],
        *parts, step_c, c, sum_t, gram_ab,
    )
    parts = sum_parts(to_col, "col")
    (grad_b,) = call(
        second_b_kernel, [(b.shape, F32)], tensor, a, b, c, flops=2 * tensor.size * rank
    )
    weight, radix = first_digit("row")
    to_row = call(
        functools.partial(shares_kernel, len(parts), factor_b.shape[0], weight),
        messages(depth, rows_j, rank, radix),
        *parts, a, grad_b,
    )
    weight, radix = first_digit("col")
    to_col = call(
        functools.partial(second_a_kernel, weight, factor_a.shape[0]),
        messages(0, rows_i, rank, radix),
        tensor, a, b, c,
        scratch=[pltpu.VMEM((rows_i, rank), F32)],
        flops=2 * tensor.size * rank,
    )
    rows, to_col = sum_shares(to_row, "row", factor_b.shape[0], depth, to_col)
    cols = sum_shares(to_col, "col", factor_a.shape[0], 0)
    return call(
        functools.partial(last_kernel, len(rows), len(cols)),
        [(factor_a.shape, F32), (factor_b.shape, F32), (c.shape, F32)],
        *rows, *cols, a, b, c,
        hbm_out=True,
    )


def solution(mesh):
    return jax.shard_map(
        local,
        mesh=mesh,
        in_specs=(P("row", "col", None), P(("row", "col"), None), P(("col", "row"), None), P()),
        out_specs=(P(("row", "col"), None), P(("col", "row"), None), P()),
        check_vma=False,
    )
```

```python
import functools

import jax
import jax.numpy as jnp
from jax import lax
from jax.experimental import pallas as pl
from jax.experimental.pallas import tpu as pltpu
from jax.sharding import PartitionSpec as P

F32 = jnp.float32
BF16 = jnp.bfloat16
NORM_ROWS = 16
VMEM_LIMIT = 4 << 20
HOLD_FLOPS = 5 * 10**9
PLACE_FLOPS = 2 * 10**9


damping = 0.9
scaling = 0.25
epsilon = 1e-06


def vmem(x):
    return pltpu.with_memory_space_constraint(x, pltpu.VMEM)


def call(body, outs, *operands, scratch=(), hbm_out=False, flops=0):
    whole = pl.BlockSpec(memory_space=pltpu.VMEM)
    place = jax.ShapeDtypeStruct if hbm_out else pltpu.VMEM
    return pl.pallas_call(
        body,
        in_specs=[whole] * len(operands),
        out_specs=[whole] * len(outs),
        out_shape=[place(s, d) for s, d in outs],
        scratch_shapes=scratch,
        cost_estimate=pl.CostEstimate(flops=flops, bytes_accessed=0, transcendentals=0),
        compiler_params=pltpu.CompilerParams(vmem_limit_bytes=VMEM_LIMIT),
    )(*[vmem(x) for x in operands])


def divisor(n, most):
    return next(g for g in (256, 128, 64, 32, 16, 8, 4, 2) if g <= most and n % g == 0)


def dot(x, y):
    return jnp.dot(x, y, preferred_element_type=F32)


def dot_rows(x, y):
    return lax.dot_general(x, y, (((0,), (0,)), ((), ())), preferred_element_type=F32)


def gram(x16):
    return dot_rows(x16, x16)


def dot_wide(x16, y):
    high = y.astype(BF16)
    low = (y - high.astype(F32)).astype(BF16)
    return dot(x16, high) + dot(x16, low)


def put_norm(ref, start, norm):
    high = norm.astype(BF16).astype(F32)
    rest = norm - high
    mid = rest.astype(BF16).astype(F32)
    low = rest - mid
    rows = jnp.concatenate([high, mid, low, jnp.zeros((NORM_ROWS - 3, norm.shape[1]), F32)], 0)
    ref[start : start + NORM_ROWS] = rows.astype(ref.dtype)


def get_norm(ref, start):
    rows = ref[start : start + NORM_ROWS].astype(F32)
    return rows[0:1] + rows[1:2] + rows[2:3]


def squares(x16):
    return jnp.sum(jnp.square(x16.astype(F32)), axis=0, keepdims=True)


def tree(parts):
    while len(parts) > 1:
        parts = [parts[q] + parts[q + 1] for q in range(0, len(parts), 2)]
    return parts[0]


def sum_rows(refs, start, rows):
    return tree([r[start : start + rows].astype(F32) for r in refs])


def sum_norm(refs, start):
    return tree([get_norm(r, start) for r in refs])


def digits(n):
    weight = 1
    while weight < n:
        radix = 4 if (n // weight) % 4 == 0 else 2
        yield weight, radix
        weight *= radix


def digit_of(axis, weight, radix):
    return lax.rem(lax.div(lax.axis_index(axis), weight), radix)


def swap(x, axis, weight, q):
    return lax.ppermute(x, axis, [(i, i ^ (q * weight)) for i in range(lax.axis_size(axis))])


def turns(radix):
    return [0] + list(range(radix - 1, 0, -1))


def twice(c16):
    zero = jnp.zeros_like(c16)
    return jnp.concatenate(
        [jnp.concatenate([c16, zero], 1), jnp.concatenate([zero, c16], 1)], 0
    )


def place_kernel(axis, weight, *refs):
    *ins, out = refs
    rows = ins[0].shape[0]
    digit = digit_of(axis, weight, len(ins))
    for q, ref in zip(turns(len(ins)), ins):
        out[pl.ds(pl.multiple_of((digit ^ q) * rows, rows), rows)] = ref[...]


def gather_digit(x, own, axis, weight, radix):
    got = [swap(x, axis, weight, q) for q in turns(radix)[1:]]
    (x,) = call(
        functools.partial(place_kernel, axis, weight),
        [((x.shape[0] * radix, x.shape[1]), x.dtype)],
        own, *got,
        flops=PLACE_FLOPS,
    )
    return x


def gather(x, own, axis):
    for weight, radix in digits(lax.axis_size(axis)):
        x = own = gather_digit(x, own, axis, weight, radix)
    return x


def hold_kernel(*refs):
    half = len(refs) // 2
    for ref, out in zip(refs[:half], refs[half:]):
        out[...] = ref[...]


def hold(*arrays):
    whole = pl.BlockSpec(memory_space=pltpu.VMEM)
    return pl.pallas_call(
        hold_kernel,
        out_specs=[whole] * len(arrays),
        out_shape=[pltpu.VMEM(x.shape, x.dtype) for x in arrays],
        cost_estimate=pl.CostEstimate(flops=HOLD_FLOPS, bytes_accessed=0, transcendentals=0),
    )(*[pltpu.with_memory_space_constraint(x, pltpu.HBM) for x in arrays])


def add_kernel(norm_at, *refs):
    *ins, out = refs
    out[...] = sum_rows(ins, 0, out.shape[0]).astype(BF16)
    if norm_at is not None:
        put_norm(out, norm_at, sum_norm(ins, norm_at))


def sum_parts(x, axis, norm_at=None, high_first=False):
    parts = [x]
    order = list(digits(lax.axis_size(axis)))
    for weight, radix in reversed(order) if high_first else order:
        if len(parts) > 1:
            (x,) = call(functools.partial(add_kernel, norm_at), [(x.shape, BF16)], *parts)
        parts = [x] + [swap(x, axis, weight, q) for q in turns(radix)[1:]]
    return parts


def sum_c(t_ref, a_ref, b16, acc):
    rows_i, rows_j, depth = t_ref.shape
    group = divisor(rows_i, 256)
    acc[...] = jnp.zeros_like(acc)

    def step(g, carry):
        at = pl.ds(pl.multiple_of(g * group, group), group)
        a16 = a_ref[at].astype(BF16)
        pairs = jnp.concatenate([a16[q : q + 1] * b16 for q in range(group)], 0)
        acc[...] += dot_rows(t_ref[at].reshape(group * rows_j, depth), pairs)
        return carry

    lax.fori_loop(0, rows_i // group, step, 0)


def sum_b(t_ref, a_ref, c16, acc, low, high):
    rows_i, rows_j, depth = t_ref.shape
    rank = c16.shape[1]
    half = rows_i // 2
    group = divisor(half, 128)
    pair_c = twice(c16)
    acc[...] = jnp.zeros_like(acc)

    def step(g, carry):
        first = pl.multiple_of(g * group, group)
        left, right = t_ref[pl.ds(first, group)], t_ref[pl.ds(half + first, group)]
        a_left = a_ref[pl.ds(first, group)].astype(BF16).astype(F32)
        a_right = a_ref[pl.ds(half + first, group)].astype(BF16).astype(F32)
        total = acc[...]
        for q in range(group):
            along = dot(jnp.concatenate([left[q], right[q]], 1), pair_c)
            for part, kept, a32 in ((along[:, :rank], low, a_left), (along[:, rank:], high, a_right)):
                kept[first + q] = part
                total = total + part * a32[q : q + 1]
        acc[...] = total
        return carry

    lax.fori_loop(0, half // group, step, 0)


def sum_a(low, high, b16, acc):
    half = low.shape[0]
    group = divisor(half, 128)
    b32 = b16.astype(F32)

    def step(g, carry):
        first = pl.multiple_of(g * group, group)
        for start, kept in ((first, low), (half + first, high)):
            sums = [jnp.sum(kept[first + q] * b32, axis=0, keepdims=True) for q in range(group)]
            acc[pl.ds(start, group)] = jnp.concatenate(sums, 0)
        return carry

    lax.fori_loop(0, half // group, step, 0)


def kept_shapes(tensor, rank):
    rows_i, rows_j, _ = tensor.shape
    return [((rows_i // 2, rows_j, rank), F32)] * 2


def first_b_kernel(t_ref, a_ref, c_ref, acc, low, high):
    sum_b(t_ref, a_ref, c_ref[...].astype(BF16), acc, low, high)


def first_c_kernel(t_ref, a_ref, b_ref, c_ref, acc_b, row_ref, acc_c):
    rows_j, depth = b_ref.shape[0], c_ref.shape[0]
    a16 = a_ref[...].astype(BF16)
    b16 = b_ref[...].astype(BF16)
    c16 = c_ref[...].astype(BF16)
    sum_c(t_ref, a_ref, b16, acc_c)
    gram_a, gram_b, gram_c = gram(a16), gram(b16), gram(c16)
    row_ref[:rows_j] = (acc_b[...] - dot_wide(b16, gram_a * gram_c)).astype(BF16)
    row_ref[rows_j : rows_j + depth] = (acc_c[...] - dot_wide(c16, gram_a * gram_b)).astype(BF16)
    put_norm(row_ref, rows_j + depth, squares(a16))


def first_a_kernel(low, high, a_ref, b_ref, c_ref, col_ref, acc_a):
    rows_i = a_ref.shape[0]
    b16 = b_ref[...].astype(BF16)
    sum_a(low, high, b16, acc_a)
    model = dot_wide(a_ref[...].astype(BF16), gram(b16) * gram(c_ref[...].astype(BF16)))
    col_ref[:rows_i] = (acc_a[...] - model).astype(BF16)
    put_norm(col_ref, rows_i, squares(b16))


def middle_kernel(n_row, n_col, *refs):
    rows, refs = refs[:n_row], refs[n_row:]
    cols, refs = refs[:n_col], refs[n_col:]
    a_ref, b_ref, c_ref, new_a, new_b, part_c, step_c = refs
    rows_i, rows_j, depth = a_ref.shape[0], b_ref.shape[0], c_ref.shape[0]
    norm_a = sum_norm(rows, rows_j + depth)
    norm_b = sum_norm(cols, rows_i)
    norm_c = squares(c_ref[...].astype(BF16))
    step_a = scaling / (norm_b * norm_c + epsilon)
    step_b = scaling / (norm_a * norm_c + epsilon)
    new_a[...] = damping * a_ref[...] + step_a * sum_rows(cols, 0, rows_i)
    new_b[...] = damping * b_ref[...] + step_b * sum_rows(rows, 0, rows_j)
    part_c[...] = sum_rows(rows, rows_j, depth).astype(BF16)
    step_c[...] = jnp.broadcast_to(scaling / (norm_a * norm_b + epsilon), step_c.shape)


def second_c_kernel(t_ref, a_ref, b_ref, sum_ref, gram_ref):
    a16 = a_ref[...].astype(BF16)
    b16 = b_ref[...].astype(BF16)
    sum_c(t_ref, a_ref, b16, sum_ref)
    gram_ref[...] = gram(a16) * gram(b16)


def second_model_kernel(n_col, *refs):
    parts, refs = refs[:n_col], refs[n_col:]
    step_ref, c_ref, sum_ref, gram_ref, new_c, out_ref = refs
    c2 = damping * c_ref[...] + step_ref[0:1] * sum_rows(parts, 0, c_ref.shape[0])
    new_c[...] = c2
    out_ref[...] = (sum_ref[...] - dot_wide(c2.astype(BF16), gram_ref[...])).astype(BF16)


def second_b_kernel(t_ref, a_ref, b_ref, c_ref, grad_b, low, high):
    a16 = a_ref[...].astype(BF16)
    c16 = c_ref[...].astype(BF16)
    sum_b(t_ref, a_ref, c16, grad_b, low, high)
    grad_b[...] -= dot_wide(b_ref[...].astype(BF16), gram(a16) * gram(c16))


def second_a_kernel(weight, own_i, low, high, a_ref, b_ref, c_ref, *refs):
    *outs, acc_a = refs
    b16 = b_ref[...].astype(BF16)
    sum_a(low, high, b16, acc_a)
    acc_a[...] -= dot_wide(a_ref[...].astype(BF16), gram(b16) * gram(c_ref[...].astype(BF16)))
    put_shares("col", weight, own_i, None, squares(b16), acc_a, outs)


def put_shares(axis, weight, own, shared, norm, grad, outs):
    radix = len(outs)
    depth = 0 if shared is None else shared.shape[0]
    blocks = grad.shape[0] // own
    digit = digit_of(axis, weight, radix)
    for q, out in zip(turns(radix), outs):
        if depth:
            out[:depth] = shared
        put_norm(out, depth, norm)
        first = [(high * radix + (digit ^ q)) * own for high in range(blocks // radix)]
        rows = [grad[pl.ds(pl.multiple_of(at, own), own)] for at in first]
        out[depth + NORM_ROWS :] = jnp.concatenate(rows, 0).astype(out.dtype)


def shares_kernel(n_col, own_j, weight, *refs):
    parts, refs = refs[:n_col], refs[n_col:]
    a_ref, grad_b, outs = refs[0], refs[1], refs[2:]
    shared = sum_rows(parts, 0, parts[0].shape[0]).astype(BF16)
    put_shares("row", weight, own_j, shared, squares(a_ref[...].astype(BF16)), grad_b, outs)


def next_shares_kernel(axis, weight, own, depth, n_parts, *refs):
    parts, outs, grad = refs[:n_parts], refs[n_parts:-1], refs[-1]
    shared = sum_rows(parts, 0, depth).astype(BF16) if depth else None
    grad[...] = sum_rows(parts, depth + NORM_ROWS, grad.shape[0])
    put_shares(axis, weight, own, shared, sum_norm(parts, depth), grad, outs)


def first_digit(axis):
    return next(digits(lax.axis_size(axis)))


def messages(depth, rows, rank, radix, dtype):
    return [((depth + NORM_ROWS + rows // radix, rank), dtype)] * radix


def sum_shares(sent, axis, own, depth, beside=None):
    rank = sent[0].shape[1]
    parts = None
    for weight, radix in digits(lax.axis_size(axis)):
        if parts is not None:
            held = parts[0].shape[0] - depth - NORM_ROWS
            sent = call(
                functools.partial(next_shares_kernel, axis, weight, own, depth, len(parts)),
                messages(depth, held, rank, radix, sent[0].dtype),
                *parts,
                scratch=[pltpu.VMEM((held, rank), F32)],
            )
            if beside is not None:
                sent, _ = lax.optimization_barrier((sent, beside))
        got = [swap(x, axis, weight, q) for q, x in zip(turns(radix)[1:], sent[1:])]
        parts = [sent[0]] + got
    return parts


def last_kernel(n_row, n_col, *refs):
    rows, refs = refs[:n_row], refs[n_row:]
    cols, refs = refs[:n_col], refs[n_col:]
    a_ref, b_ref, c_ref, out_a, out_b, out_c = refs
    depth = c_ref.shape[0]
    own_i, own_j = out_a.shape[0], out_b.shape[0]
    norm_a = sum_norm(rows, depth)
    norm_b = sum_norm(cols, 0)
    norm_c = squares(c_ref[...].astype(BF16))
    step_a = scaling / (norm_b * norm_c + epsilon)
    step_b = scaling / (norm_a * norm_c + epsilon)
    step_c = scaling / (norm_a * norm_b + epsilon)
    at_i = pl.ds(pl.multiple_of(lax.axis_index("col") * own_i, own_i), own_i)
    at_j = pl.ds(pl.multiple_of(lax.axis_index("row") * own_j, own_j), own_j)
    out_a[...] = damping * a_ref[at_i] + step_a * sum_rows(cols, NORM_ROWS, own_i)
    out_b[...] = damping * b_ref[at_j] + step_b * sum_rows(rows, depth + NORM_ROWS, own_j)
    out_c[...] = damping * c_ref[...] + step_c * sum_rows(rows, 0, depth)


def local(tensor, factor_a, factor_b, factor_c):
    rows_i, rows_j, depth = tensor.shape
    rank = factor_a.shape[1]
    held_a, held_b, c = hold(factor_a, factor_b, factor_c)
    b = gather(factor_b, held_b, "row")
    a = gather(held_a, held_a, "col")

    kept = kept_shapes(tensor, rank)
    grad_b, low, high = call(
        first_b_kernel, [(b.shape, F32)] + kept, tensor, a, c, flops=2 * tensor.size * rank
    )
    (to_row,) = call(
        first_c_kernel,
        [((rows_j + depth + NORM_ROWS, rank), BF16)],
        tensor, a, b, c, grad_b,
        scratch=[pltpu.VMEM(c.shape, F32)],
        flops=2 * tensor.size * rank,
    )
    (to_col,) = call(
        first_a_kernel,
        [((rows_i + NORM_ROWS, rank), BF16)],
        low, high, a, b, c,
        scratch=[pltpu.VMEM(a.shape, F32)],
        flops=tensor.size * rank,
    )
    rows = sum_parts(to_row, "row", rows_j + depth, high_first=True)
    cols = sum_parts(to_col, "col", rows_i)
    a, b, part_c, step_c = call(
        functools.partial(middle_kernel, len(rows), len(cols)),
        [(a.shape, F32), (b.shape, F32), (c.shape, BF16), ((8, rank), F32)],
        *rows, *cols, a, b, c,
    )

    parts = sum_parts(part_c, "col")
    sum_t, gram_ab = call(
        second_c_kernel,
        [(c.shape, F32), ((rank, rank), F32)],
        tensor, a, b,
        flops=2 * tensor.size * rank,
    )
    c, to_col = call(
        functools.partial(second_model_kernel, len(parts)),
        [(c.shape, F32), (c.shape, BF16)],
        *parts, step_c, c, sum_t, gram_ab,
    )
    parts = sum_parts(to_col, "col")
    grad_b, low, high = call(
        second_b_kernel, [(b.shape, F32)] + kept, tensor, a, b, c, flops=2 * tensor.size * rank
    )
    weight, radix = first_digit("row")
    to_row = call(
        functools.partial(shares_kernel, len(parts), factor_b.shape[0], weight),
        messages(depth, rows_j, rank, radix, BF16),
        *parts, a, grad_b,
    )
    weight, radix = first_digit("col")
    to_col = call(
        functools.partial(second_a_kernel, weight, factor_a.shape[0]),
        messages(0, rows_i, rank, radix, F32),
        low, high, a, b, c,
        scratch=[pltpu.VMEM((rows_i, rank), F32)],
        flops=tensor.size * rank,
    )
    rows = sum_shares(to_row, "row", factor_b.shape[0], depth, to_col)
    cols = sum_shares(to_col, "col", factor_a.shape[0], 0)
    return call(
        functools.partial(last_kernel, len(rows), len(cols)),
        [(factor_a.shape, F32), (factor_b.shape, F32), (c.shape, F32)],
        *rows, *cols, a, b, c,
        hbm_out=True,
    )


def solution(mesh):
    return jax.shard_map(
        local,
        mesh=mesh,
        in_specs=(P("row", "col", None), P(("row", "col"), None), P(("col", "row"), None), P()),
        out_specs=(P(("row", "col"), None), P(("col", "row"), None), P()),
        check_vma=False,
    )
```

```python
import functools

import jax
import jax.numpy as jnp
from jax import lax
from jax.experimental import pallas as pl
from jax.experimental.pallas import tpu as pltpu
from jax.sharding import PartitionSpec as P

F32 = jnp.float32
BF16 = jnp.bfloat16
NORM_ROWS = 16
VMEM_LIMIT = 4 << 20
HOLD_FLOPS = 5 * 10**9
PLACE_FLOPS = 2 * 10**9


damping = 0.9
scaling = 0.25
epsilon = 1e-06


def vmem(x):
    return pltpu.with_memory_space_constraint(x, pltpu.VMEM)


def call(body, outs, *operands, scratch=(), hbm_out=False, flops=0):
    whole = pl.BlockSpec(memory_space=pltpu.VMEM)
    place = jax.ShapeDtypeStruct if hbm_out else pltpu.VMEM
    return pl.pallas_call(
        body,
        in_specs=[whole] * len(operands),
        out_specs=[whole] * len(outs),
        out_shape=[place(s, d) for s, d in outs],
        scratch_shapes=scratch,
        cost_estimate=pl.CostEstimate(flops=flops, bytes_accessed=0, transcendentals=0),
        compiler_params=pltpu.CompilerParams(vmem_limit_bytes=VMEM_LIMIT),
    )(*[vmem(x) for x in operands])


def divisor(n, most):
    return next(g for g in (256, 128, 64, 32, 16, 8, 4, 2) if g <= most and n % g == 0)


def dot(x, y):
    return jnp.dot(x, y, preferred_element_type=F32)


def dot_rows(x, y):
    return lax.dot_general(x, y, (((0,), (0,)), ((), ())), preferred_element_type=F32)


def gram(x16):
    return dot_rows(x16, x16)


def dot_wide(x16, y):
    high = y.astype(BF16)
    low = (y - high.astype(F32)).astype(BF16)
    return dot(x16, high) + dot(x16, low)


def put_norm(ref, start, norm):
    high = norm.astype(BF16).astype(F32)
    rest = norm - high
    mid = rest.astype(BF16).astype(F32)
    low = rest - mid
    rows = jnp.concatenate([high, mid, low, jnp.zeros((NORM_ROWS - 3, norm.shape[1]), F32)], 0)
    ref[start : start + NORM_ROWS] = rows.astype(ref.dtype)


def get_norm(ref, start):
    rows = ref[start : start + NORM_ROWS].astype(F32)
    return rows[0:1] + rows[1:2] + rows[2:3]


def squares(x16):
    return jnp.sum(jnp.square(x16.astype(F32)), axis=0, keepdims=True)


def tree(parts):
    while len(parts) > 1:
        parts = [parts[q] + parts[q + 1] for q in range(0, len(parts), 2)]
    return parts[0]


def sum_rows(refs, start, rows):
    return tree([r[start : start + rows].astype(F32) for r in refs])


def sum_norm(refs, start):
    return tree([get_norm(r, start) for r in refs])


def digits(n):
    weight = 1
    while weight < n:
        radix = 4 if (n // weight) % 4 == 0 else 2
        yield weight, radix
        weight *= radix


def digit_of(axis, weight, radix):
    return lax.rem(lax.div(lax.axis_index(axis), weight), radix)


def swap(x, axis, weight, q):
    return lax.ppermute(x, axis, [(i, i ^ (q * weight)) for i in range(lax.axis_size(axis))])


def turns(radix):
    return [0] + list(range(radix - 1, 0, -1))


def twice(c16):
    zero = jnp.zeros_like(c16)
    return jnp.concatenate(
        [jnp.concatenate([c16, zero], 1), jnp.concatenate([zero, c16], 1)], 0
    )


def place_kernel(axis, weight, *refs):
    *ins, out = refs
    rows = ins[0].shape[0]
    digit = digit_of(axis, weight, len(ins))
    for q, ref in zip(turns(len(ins)), ins):
        out[pl.ds(pl.multiple_of((digit ^ q) * rows, rows), rows)] = ref[...]


def gather_digit(x, own, axis, weight, radix):
    got = [swap(x, axis, weight, q) for q in turns(radix)[1:]]
    (x,) = call(
        functools.partial(place_kernel, axis, weight),
        [((x.shape[0] * radix, x.shape[1]), x.dtype)],
        own, *got,
        flops=PLACE_FLOPS,
    )
    return x


def gather(x, own, axis):
    for weight, radix in digits(lax.axis_size(axis)):
        x = own = gather_digit(x, own, axis, weight, radix)
    return x


def hold_kernel(*refs):
    half = len(refs) // 2
    for ref, out in zip(refs[:half], refs[half:]):
        out[...] = ref[...]


def hold(*arrays):
    whole = pl.BlockSpec(memory_space=pltpu.VMEM)
    return pl.pallas_call(
        hold_kernel,
        out_specs=[whole] * len(arrays),
        out_shape=[pltpu.VMEM(x.shape, x.dtype) for x in arrays],
        cost_estimate=pl.CostEstimate(flops=HOLD_FLOPS, bytes_accessed=0, transcendentals=0),
    )(*[pltpu.with_memory_space_constraint(x, pltpu.HBM) for x in arrays])


def add_kernel(norm_at, *refs):
    *ins, out = refs
    out[...] = sum_rows(ins, 0, out.shape[0]).astype(BF16)
    if norm_at is not None:
        put_norm(out, norm_at, sum_norm(ins, norm_at))


def sum_parts(x, axis, norm_at=None, high_first=False):
    parts = [x]
    order = list(digits(lax.axis_size(axis)))
    for weight, radix in reversed(order) if high_first else order:
        if len(parts) > 1:
            (x,) = call(functools.partial(add_kernel, norm_at), [(x.shape, BF16)], *parts)
        parts = [x] + [swap(x, axis, weight, q) for q in turns(radix)[1:]]
    return parts


def sum_c(t_ref, a_ref, b16, acc):
    rows_i, rows_j, depth = t_ref.shape
    group = divisor(rows_i, 256)
    acc[...] = jnp.zeros_like(acc)

    def step(g, carry):
        at = pl.ds(pl.multiple_of(g * group, group), group)
        a16 = a_ref[at].astype(BF16)
        pairs = jnp.concatenate([a16[q : q + 1] * b16 for q in range(group)], 0)
        acc[...] += dot_rows(t_ref[at].reshape(group * rows_j, depth), pairs)
        return carry

    lax.fori_loop(0, rows_i // group, step, 0)


def sum_b(t_ref, a_ref, c16, acc, low, high):
    rows_i, rows_j, depth = t_ref.shape
    rank = c16.shape[1]
    half = rows_i // 2
    group = divisor(half, 128)
    pair_c = twice(c16)
    acc[...] = jnp.zeros_like(acc)

    def step(g, carry):
        first = pl.multiple_of(g * group, group)
        left, right = t_ref[pl.ds(first, group)], t_ref[pl.ds(half + first, group)]
        a_left = a_ref[pl.ds(first, group)].astype(BF16).astype(F32)
        a_right = a_ref[pl.ds(half + first, group)].astype(BF16).astype(F32)
        total = acc[...]
        for q in range(group):
            along = dot(jnp.concatenate([left[q], right[q]], 1), pair_c)
            for part, kept, a32 in ((along[:, :rank], low, a_left), (along[:, rank:], high, a_right)):
                kept[first + q] = part
                total = total + part * a32[q : q + 1]
        acc[...] = total
        return carry

    lax.fori_loop(0, half // group, step, 0)


def sum_a(low, high, b16, acc):
    half = low.shape[0]
    group = divisor(half, 128)
    b32 = b16.astype(F32)

    def step(g, carry):
        first = pl.multiple_of(g * group, group)
        for start, kept in ((first, low), (half + first, high)):
            sums = [jnp.sum(kept[first + q] * b32, axis=0, keepdims=True) for q in range(group)]
            acc[pl.ds(start, group)] = jnp.concatenate(sums, 0)
        return carry

    lax.fori_loop(0, half // group, step, 0)


def kept_shapes(tensor, rank):
    rows_i, rows_j, _ = tensor.shape
    return [((rows_i // 2, rows_j, rank), F32)] * 2


def first_b_kernel(t_ref, a_ref, c_ref, acc, low, high):
    sum_b(t_ref, a_ref, c_ref[...].astype(BF16), acc, low, high)


def first_c_kernel(t_ref, a_ref, b_ref, c_ref, acc_b, row_ref, acc_c):
    rows_j, depth = b_ref.shape[0], c_ref.shape[0]
    a16 = a_ref[...].astype(BF16)
    b16 = b_ref[...].astype(BF16)
    c16 = c_ref[...].astype(BF16)
    sum_c(t_ref, a_ref, b16, acc_c)
    gram_a, gram_b, gram_c = gram(a16), gram(b16), gram(c16)
    row_ref[:rows_j] = (acc_b[...] - dot_wide(b16, gram_a * gram_c)).astype(BF16)
    row_ref[rows_j : rows_j + depth] = (acc_c[...] - dot_wide(c16, gram_a * gram_b)).astype(BF16)
    put_norm(row_ref, rows_j + depth, squares(a16))


def first_a_kernel(low, high, a_ref, b_ref, c_ref, col_ref, acc_a):
    rows_i = a_ref.shape[0]
    b16 = b_ref[...].astype(BF16)
    sum_a(low, high, b16, acc_a)
    model = dot_wide(a_ref[...].astype(BF16), gram(b16) * gram(c_ref[...].astype(BF16)))
    col_ref[:rows_i] = (acc_a[...] - model).astype(BF16)
    put_norm(col_ref, rows_i, squares(b16))


def new_a_kernel(n_col, *refs):
    cols, refs = refs[:n_col], refs[n_col:]
    a_ref, c_ref, new_a, gram_a = refs
    rows_i = a_ref.shape[0]
    norm_c = squares(c_ref[...].astype(BF16))
    step_a = scaling / (sum_norm(cols, rows_i) * norm_c + epsilon)
    a2 = damping * a_ref[...] + step_a * sum_rows(cols, 0, rows_i)
    new_a[...] = a2
    gram_a[...] = gram(a2.astype(BF16))


def middle_kernel(n_row, n_col, *refs):
    rows, refs = refs[:n_row], refs[n_row:]
    cols, refs = refs[:n_col], refs[n_col:]
    b_ref, c_ref, new_b, part_c, step_c = refs
    rows_j, depth = b_ref.shape[0], c_ref.shape[0]
    norm_a = sum_norm(rows, rows_j + depth)
    norm_b = sum_norm(cols, cols[0].shape[0] - NORM_ROWS)
    norm_c = squares(c_ref[...].astype(BF16))
    step_b = scaling / (norm_a * norm_c + epsilon)
    new_b[...] = damping * b_ref[...] + step_b * sum_rows(rows, 0, rows_j)
    part_c[...] = sum_rows(rows, rows_j, depth).astype(BF16)
    step_c[...] = jnp.broadcast_to(scaling / (norm_a * norm_b + epsilon), step_c.shape)


def second_c_kernel(t_ref, a_ref, b_ref, gram_a, sum_ref, gram_ref):
    b16 = b_ref[...].astype(BF16)
    sum_c(t_ref, a_ref, b16, sum_ref)
    gram_ref[...] = gram_a[...] * gram(b16)


def second_model_kernel(n_col, *refs):
    parts, refs = refs[:n_col], refs[n_col:]
    step_ref, c_ref, sum_ref, gram_ref, new_c, out_ref = refs
    c2 = damping * c_ref[...] + step_ref[0:1] * sum_rows(parts, 0, c_ref.shape[0])
    new_c[...] = c2
    out_ref[...] = (sum_ref[...] - dot_wide(c2.astype(BF16), gram_ref[...])).astype(BF16)


def second_b_kernel(t_ref, a_ref, b_ref, c_ref, gram_a, grad_b, low, high):
    c16 = c_ref[...].astype(BF16)
    sum_b(t_ref, a_ref, c16, grad_b, low, high)
    grad_b[...] -= dot_wide(b_ref[...].astype(BF16), gram_a[...] * gram(c16))


def second_a_kernel(weight, own_i, low, high, a_ref, b_ref, c_ref, *refs):
    *outs, acc_a = refs
    b16 = b_ref[...].astype(BF16)
    sum_a(low, high, b16, acc_a)
    acc_a[...] -= dot_wide(a_ref[...].astype(BF16), gram(b16) * gram(c_ref[...].astype(BF16)))
    put_shares("col", weight, own_i, None, squares(b16), acc_a, outs)


def put_shares(axis, weight, own, shared, norm, grad, outs):
    radix = len(outs)
    depth = 0 if shared is None else shared.shape[0]
    blocks = grad.shape[0] // own
    digit = digit_of(axis, weight, radix)
    for q, out in zip(turns(radix), outs):
        if depth:
            out[:depth] = shared
        put_norm(out, depth, norm)
        first = [(high * radix + (digit ^ q)) * own for high in range(blocks // radix)]
        rows = [grad[pl.ds(pl.multiple_of(at, own), own)] for at in first]
        out[depth + NORM_ROWS :] = jnp.concatenate(rows, 0).astype(out.dtype)


def shares_kernel(n_col, own_j, weight, *refs):
    parts, refs = refs[:n_col], refs[n_col:]
    a_ref, grad_b, outs = refs[0], refs[1], refs[2:]
    shared = sum_rows(parts, 0, parts[0].shape[0]).astype(BF16)
    put_shares("row", weight, own_j, shared, squares(a_ref[...].astype(BF16)), grad_b, outs)


def next_shares_kernel(axis, weight, own, depth, n_parts, *refs):
    parts, outs, grad = refs[:n_parts], refs[n_parts:-1], refs[-1]
    shared = sum_rows(parts, 0, depth).astype(BF16) if depth else None
    grad[...] = sum_rows(parts, depth + NORM_ROWS, grad.shape[0])
    put_shares(axis, weight, own, shared, sum_norm(parts, depth), grad, outs)


def first_digit(axis):
    return next(digits(lax.axis_size(axis)))


def messages(depth, rows, rank, radix, dtype):
    return [((depth + NORM_ROWS + rows // radix, rank), dtype)] * radix


def sum_shares(sent, axis, own, depth, beside=None):
    rank = sent[0].shape[1]
    parts = None
    for weight, radix in digits(lax.axis_size(axis)):
        if parts is not None:
            held = parts[0].shape[0] - depth - NORM_ROWS
            sent = call(
                functools.partial(next_shares_kernel, axis, weight, own, depth, len(parts)),
                messages(depth, held, rank, radix, sent[0].dtype),
                *parts,
                scratch=[pltpu.VMEM((held, rank), F32)],
            )
            if beside is not None:
                sent, _ = lax.optimization_barrier((sent, beside))
        got = [swap(x, axis, weight, q) for q, x in zip(turns(radix)[1:], sent[1:])]
        parts = [sent[0]] + got
    return parts


def last_a_kernel(n_col, *refs):
    cols, refs = refs[:n_col], refs[n_col:]
    a_ref, c_ref, out_a = refs
    own_i = out_a.shape[0]
    norm_c = squares(c_ref[...].astype(BF16))
    step_a = scaling / (sum_norm(cols, 0) * norm_c + epsilon)
    at_i = pl.ds(pl.multiple_of(lax.axis_index("col") * own_i, own_i), own_i)
    out_a[...] = damping * a_ref[at_i] + step_a * sum_rows(cols, NORM_ROWS, own_i)


def last_kernel(n_row, n_col, *refs):
    rows, refs = refs[:n_row], refs[n_row:]
    cols, refs = refs[:n_col], refs[n_col:]
    b_ref, c_ref, out_b, out_c = refs
    depth = c_ref.shape[0]
    own_j = out_b.shape[0]
    norm_a = sum_norm(rows, depth)
    norm_b = sum_norm(cols, 0)
    norm_c = squares(c_ref[...].astype(BF16))
    step_b = scaling / (norm_a * norm_c + epsilon)
    step_c = scaling / (norm_a * norm_b + epsilon)
    at_j = pl.ds(pl.multiple_of(lax.axis_index("row") * own_j, own_j), own_j)
    out_b[...] = damping * b_ref[at_j] + step_b * sum_rows(rows, depth + NORM_ROWS, own_j)
    out_c[...] = damping * c_ref[...] + step_c * sum_rows(rows, 0, depth)


def local(tensor, factor_a, factor_b, factor_c):
    rows_i, rows_j, depth = tensor.shape
    rank = factor_a.shape[1]
    held_a, held_b, c = hold(factor_a, factor_b, factor_c)
    b = gather(factor_b, held_b, "row")
    a = gather(held_a, held_a, "col")

    kept = kept_shapes(tensor, rank)
    grad_b, low, high = call(
        first_b_kernel, [(b.shape, F32)] + kept, tensor, a, c, flops=2 * tensor.size * rank
    )
    (to_row,) = call(
        first_c_kernel,
        [((rows_j + depth + NORM_ROWS, rank), BF16)],
        tensor, a, b, c, grad_b,
        scratch=[pltpu.VMEM(c.shape, F32)],
        flops=2 * tensor.size * rank,
    )
    (to_col,) = call(
        first_a_kernel,
        [((rows_i + NORM_ROWS, rank), BF16)],
        low, high, a, b, c,
        scratch=[pltpu.VMEM(a.shape, F32)],
        flops=tensor.size * rank,
    )
    rows = sum_parts(to_row, "row", rows_j + depth, high_first=True)
    cols = sum_parts(to_col, "col", rows_i)
    a, gram_a = call(
        functools.partial(new_a_kernel, len(cols)),
        [(a.shape, F32), ((rank, rank), F32)],
        *cols, a, c,
    )
    b, part_c, step_c = call(
        functools.partial(middle_kernel, len(rows), len(cols)),
        [(b.shape, F32), (c.shape, BF16), ((8, rank), F32)],
        *rows, *cols, b, c,
    )

    parts = sum_parts(part_c, "col")
    sum_t, gram_ab = call(
        second_c_kernel,
        [(c.shape, F32), ((rank, rank), F32)],
        tensor, a, b, gram_a,
        flops=2 * tensor.size * rank,
    )
    c, to_col = call(
        functools.partial(second_model_kernel, len(parts)),
        [(c.shape, F32), (c.shape, BF16)],
        *parts, step_c, c, sum_t, gram_ab,
    )
    parts = sum_parts(to_col, "col")
    grad_b, low, high = call(
        second_b_kernel, [(b.shape, F32)] + kept, tensor, a, b, c, gram_a, flops=2 * tensor.size * rank
    )
    weight, radix = first_digit("row")
    to_row = call(
        functools.partial(shares_kernel, len(parts), factor_b.shape[0], weight),
        messages(depth, rows_j, rank, radix, BF16),
        *parts, a, grad_b,
    )
    weight, radix = first_digit("col")
    to_col = call(
        functools.partial(second_a_kernel, weight, factor_a.shape[0]),
        messages(0, rows_i, rank, radix, F32),
        low, high, a, b, c,
        scratch=[pltpu.VMEM((rows_i, rank), F32)],
        flops=tensor.size * rank,
    )
    rows = sum_shares(to_row, "row", factor_b.shape[0], depth, to_col)
    cols = sum_shares(to_col, "col", factor_a.shape[0], 0)
    (out_a,) = call(
        functools.partial(last_a_kernel, len(cols)),
        [(factor_a.shape, F32)],
        *cols, a, c,
        hbm_out=True,
    )
    out_b, out_c = call(
        functools.partial(last_kernel, len(rows), len(cols)),
        [(factor_b.shape, F32), (c.shape, F32)],
        *rows, *cols, b, c,
        hbm_out=True,
    )
    return (out_a, out_b, out_c)


def solution(mesh):
    return jax.shard_map(
        local,
        mesh=mesh,
        in_specs=(P("row", "col", None), P(("row", "col"), None), P(("col", "row"), None), P()),
        out_specs=(P(("row", "col"), None), P(("col", "row"), None), P()),
        check_vma=False,
    )
```

```python
import functools

import jax
import jax.numpy as jnp
from jax import lax
from jax.experimental import pallas as pl
from jax.experimental.pallas import tpu as pltpu
from jax.sharding import PartitionSpec as P

F32 = jnp.float32
BF16 = jnp.bfloat16
NORM_ROWS = 16
VMEM_LIMIT = 4 << 20
HOLD_FLOPS = 5 * 10**9
PLACE_FLOPS = 2 * 10**9


damping = 0.9
scaling = 0.25
epsilon = 1e-06


def vmem(x):
    return pltpu.with_memory_space_constraint(x, pltpu.VMEM)


def call(body, outs, *operands, scratch=(), hbm_out=False, flops=0):
    whole = pl.BlockSpec(memory_space=pltpu.VMEM)
    place = jax.ShapeDtypeStruct if hbm_out else pltpu.VMEM
    return pl.pallas_call(
        body,
        in_specs=[whole] * len(operands),
        out_specs=[whole] * len(outs),
        out_shape=[place(s, d) for s, d in outs],
        scratch_shapes=scratch,
        cost_estimate=pl.CostEstimate(flops=flops, bytes_accessed=0, transcendentals=0),
        compiler_params=pltpu.CompilerParams(vmem_limit_bytes=VMEM_LIMIT),
    )(*[vmem(x) for x in operands])


def divisor(n, most):
    return next(g for g in (256, 128, 64, 32, 16, 8, 4, 2) if g <= most and n % g == 0)


def dot(x, y):
    return jnp.dot(x, y, preferred_element_type=F32)


def dot_rows(x, y):
    return lax.dot_general(x, y, (((0,), (0,)), ((), ())), preferred_element_type=F32)


def gram(x16):
    return dot_rows(x16, x16)


def dot_wide(x16, y):
    high = y.astype(BF16)
    low = (y - high.astype(F32)).astype(BF16)
    return dot(x16, high) + dot(x16, low)


def put_norm(ref, start, norm):
    high = norm.astype(BF16).astype(F32)
    rest = norm - high
    mid = rest.astype(BF16).astype(F32)
    low = rest - mid
    rows = jnp.concatenate([high, mid, low, jnp.zeros((NORM_ROWS - 3, norm.shape[1]), F32)], 0)
    ref[start : start + NORM_ROWS] = rows.astype(ref.dtype)


def get_norm(ref, start):
    rows = ref[start : start + NORM_ROWS].astype(F32)
    return rows[0:1] + rows[1:2] + rows[2:3]


def squares(x16):
    return jnp.sum(jnp.square(x16.astype(F32)), axis=0, keepdims=True)


def tree(parts):
    while len(parts) > 1:
        parts = [parts[q] + parts[q + 1] for q in range(0, len(parts), 2)]
    return parts[0]


def sum_rows(refs, start, rows):
    return tree([r[start : start + rows].astype(F32) for r in refs])


def sum_norm(refs, start):
    return tree([get_norm(r, start) for r in refs])


def digits(n):
    weight = 1
    while weight < n:
        radix = 4 if (n // weight) % 4 == 0 else 2
        yield weight, radix
        weight *= radix


def digit_of(axis, weight, radix):
    return lax.rem(lax.div(lax.axis_index(axis), weight), radix)


def swap(x, axis, weight, q):
    return lax.ppermute(x, axis, [(i, i ^ (q * weight)) for i in range(lax.axis_size(axis))])


def turns(radix):
    return [0] + list(range(radix - 1, 0, -1))


def twice(c16):
    zero = jnp.zeros_like(c16)
    return jnp.concatenate(
        [jnp.concatenate([c16, zero], 1), jnp.concatenate([zero, c16], 1)], 0
    )


def place_kernel(axis, weight, *refs):
    *ins, out = refs
    rows = ins[0].shape[0]
    digit = digit_of(axis, weight, len(ins))
    for q, ref in zip(turns(len(ins)), ins):
        out[pl.ds(pl.multiple_of((digit ^ q) * rows, rows), rows)] = ref[...]


def gather_digit(x, own, axis, weight, radix):
    got = [swap(x, axis, weight, q) for q in turns(radix)[1:]]
    (x,) = call(
        functools.partial(place_kernel, axis, weight),
        [((x.shape[0] * radix, x.shape[1]), x.dtype)],
        own, *got,
        flops=PLACE_FLOPS,
    )
    return x


def gather(x, own, axis):
    for weight, radix in digits(lax.axis_size(axis)):
        x = own = gather_digit(x, own, axis, weight, radix)
    return x


def hold_kernel(*refs):
    half = len(refs) // 2
    for ref, out in zip(refs[:half], refs[half:]):
        out[...] = ref[...]


def hold(*arrays):
    whole = pl.BlockSpec(memory_space=pltpu.VMEM)
    return pl.pallas_call(
        hold_kernel,
        out_specs=[whole] * len(arrays),
        out_shape=[pltpu.VMEM(x.shape, x.dtype) for x in arrays],
        cost_estimate=pl.CostEstimate(flops=HOLD_FLOPS, bytes_accessed=0, transcendentals=0),
    )(*[pltpu.with_memory_space_constraint(x, pltpu.HBM) for x in arrays])


def add_kernel(norm_at, *refs):
    *ins, out = refs
    out[...] = sum_rows(ins, 0, out.shape[0]).astype(BF16)
    if norm_at is not None:
        put_norm(out, norm_at, sum_norm(ins, norm_at))


def sum_parts(x, axis, norm_at=None, high_first=False):
    parts = [x]
    order = list(digits(lax.axis_size(axis)))
    for weight, radix in reversed(order) if high_first else order:
        if len(parts) > 1:
            (x,) = call(functools.partial(add_kernel, norm_at), [(x.shape, BF16)], *parts)
        parts = [x] + [swap(x, axis, weight, q) for q in turns(radix)[1:]]
    return parts


def sum_c(t_ref, a_ref, b16, acc):
    rows_i, rows_j, depth = t_ref.shape
    group = divisor(rows_i, 256)
    acc[...] = jnp.zeros_like(acc)

    def step(g, carry):
        at = pl.ds(pl.multiple_of(g * group, group), group)
        a16 = a_ref[at].astype(BF16)
        pairs = jnp.concatenate([a16[q : q + 1] * b16 for q in range(group)], 0)
        acc[...] += dot_rows(t_ref[at].reshape(group * rows_j, depth), pairs)
        return carry

    lax.fori_loop(0, rows_i // group, step, 0)


def sum_b(t_ref, a_ref, c16, acc, low, high):
    rows_i, rows_j, depth = t_ref.shape
    rank = c16.shape[1]
    half = rows_i // 2
    group = divisor(half, 128)
    pair_c = twice(c16)
    acc[...] = jnp.zeros_like(acc)

    def step(g, carry):
        first = pl.multiple_of(g * group, group)
        left, right = t_ref[pl.ds(first, group)], t_ref[pl.ds(half + first, group)]
        a_left = a_ref[pl.ds(first, group)].astype(BF16).astype(F32)
        a_right = a_ref[pl.ds(half + first, group)].astype(BF16).astype(F32)
        total = acc[...]
        for q in range(group):
            along = dot(jnp.concatenate([left[q], right[q]], 1), pair_c)
            for part, kept, a32 in ((along[:, :rank], low, a_left), (along[:, rank:], high, a_right)):
                kept[first + q] = part
                total = total + part * a32[q : q + 1]
        acc[...] = total
        return carry

    lax.fori_loop(0, half // group, step, 0)


def sum_a(low, high, b16, acc):
    half = low.shape[0]
    group = divisor(half, 128)
    b32 = b16.astype(F32)

    def step(g, carry):
        first = pl.multiple_of(g * group, group)
        for start, kept in ((first, low), (half + first, high)):
            sums = [jnp.sum(kept[first + q] * b32, axis=0, keepdims=True) for q in range(group)]
            acc[pl.ds(start, group)] = jnp.concatenate(sums, 0)
        return carry

    lax.fori_loop(0, half // group, step, 0)


def kept_shapes(tensor, rank):
    rows_i, rows_j, _ = tensor.shape
    return [((rows_i // 2, rows_j, rank), F32)] * 2


def first_b_kernel(t_ref, a_ref, c_ref, acc, low, high):
    sum_b(t_ref, a_ref, c_ref[...].astype(BF16), acc, low, high)


def first_c_kernel(t_ref, a_ref, b_ref, c_ref, acc_b, row_ref, acc_c):
    rows_j, depth = b_ref.shape[0], c_ref.shape[0]
    a16 = a_ref[...].astype(BF16)
    b16 = b_ref[...].astype(BF16)
    c16 = c_ref[...].astype(BF16)
    sum_c(t_ref, a_ref, b16, acc_c)
    gram_a, gram_b, gram_c = gram(a16), gram(b16), gram(c16)
    row_ref[:rows_j] = (acc_b[...] - dot_wide(b16, gram_a * gram_c)).astype(BF16)
    row_ref[rows_j : rows_j + depth] = (acc_c[...] - dot_wide(c16, gram_a * gram_b)).astype(BF16)
    put_norm(row_ref, rows_j + depth, squares(a16))


def first_a_kernel(low, high, a_ref, b_ref, c_ref, col_ref, acc_a):
    rows_i = a_ref.shape[0]
    b16 = b_ref[...].astype(BF16)
    sum_a(low, high, b16, acc_a)
    model = dot_wide(a_ref[...].astype(BF16), gram(b16) * gram(c_ref[...].astype(BF16)))
    col_ref[:rows_i] = (acc_a[...] - model).astype(BF16)
    put_norm(col_ref, rows_i, squares(b16))


def new_a_kernel(n_col, *refs):
    cols, refs = refs[:n_col], refs[n_col:]
    a_ref, c_ref, new_a, gram_a = refs
    rows_i = a_ref.shape[0]
    norm_c = squares(c_ref[...].astype(BF16))
    step_a = scaling / (sum_norm(cols, rows_i) * norm_c + epsilon)
    a2 = damping * a_ref[...] + step_a * sum_rows(cols, 0, rows_i)
    new_a[...] = a2
    gram_a[...] = gram(a2.astype(BF16))


def middle_kernel(n_row, n_col, *refs):
    rows, refs = refs[:n_row], refs[n_row:]
    cols, refs = refs[:n_col], refs[n_col:]
    b_ref, c_ref, new_b, part_c, step_c = refs
    rows_j, depth = b_ref.shape[0], c_ref.shape[0]
    norm_a = sum_norm(rows, rows_j + depth)
    norm_b = sum_norm(cols, cols[0].shape[0] - NORM_ROWS)
    norm_c = squares(c_ref[...].astype(BF16))
    step_b = scaling / (norm_a * norm_c + epsilon)
    new_b[...] = damping * b_ref[...] + step_b * sum_rows(rows, 0, rows_j)
    part_c[...] = sum_rows(rows, rows_j, depth).astype(BF16)
    step_c[...] = jnp.broadcast_to(scaling / (norm_a * norm_b + epsilon), step_c.shape)


def second_c_kernel(t_ref, a_ref, b_ref, gram_a, sum_ref, gram_ref):
    b16 = b_ref[...].astype(BF16)
    sum_c(t_ref, a_ref, b16, sum_ref)
    gram_ref[...] = gram_a[...] * gram(b16)


def second_model_kernel(n_col, *refs):
    parts, refs = refs[:n_col], refs[n_col:]
    step_ref, c_ref, sum_ref, gram_ref, new_c, out_ref = refs
    c2 = damping * c_ref[...] + step_ref[0:1] * sum_rows(parts, 0, c_ref.shape[0])
    new_c[...] = c2
    out_ref[...] = (sum_ref[...] - dot_wide(c2.astype(BF16), gram_ref[...])).astype(BF16)


def second_b_kernel(t_ref, a_ref, b_ref, c_ref, gram_a, grad_b, low, high):
    c16 = c_ref[...].astype(BF16)
    sum_b(t_ref, a_ref, c16, grad_b, low, high)
    grad_b[...] -= dot_wide(b_ref[...].astype(BF16), gram_a[...] * gram(c16))


def second_a_kernel(weight, own_i, low, high, a_ref, b_ref, c_ref, *refs):
    *outs, acc_a = refs
    b16 = b_ref[...].astype(BF16)
    sum_a(low, high, b16, acc_a)
    acc_a[...] -= dot_wide(a_ref[...].astype(BF16), gram(b16) * gram(c_ref[...].astype(BF16)))
    put_shares("col", weight, own_i, None, squares(b16), acc_a, outs)


def put_shares(axis, weight, own, shared, norm, grad, outs):
    radix = len(outs)
    depth = 0 if shared is None else shared.shape[0]
    blocks = grad.shape[0] // own
    digit = digit_of(axis, weight, radix)
    for q, out in zip(turns(radix), outs):
        if depth:
            out[:depth] = shared
        put_norm(out, depth, norm)
        first = [(high * radix + (digit ^ q)) * own for high in range(blocks // radix)]
        rows = [grad[pl.ds(pl.multiple_of(at, own), own)] for at in first]
        out[depth + NORM_ROWS :] = jnp.concatenate(rows, 0).astype(out.dtype)


def core_rows(rows, other=False):
    core = digit_of("col", 1, 2)
    return pl.ds(pl.multiple_of(((1 - core) if other else core) * rows, rows), rows)


def shares_kernel(n_col, own_j, weight, *refs):
    parts, refs = refs[:n_col], refs[n_col:]
    a_ref, grad_b, outs, total = refs[0], refs[1], refs[2:-1], refs[-1]
    depth = total.shape[0]
    total[...] = sum_rows(parts, 0, depth)
    shared = total[core_rows(depth // 2)].astype(BF16)
    put_shares("row", weight, own_j, shared, squares(a_ref[...].astype(BF16)), grad_b, outs)


def next_shares_kernel(axis, weight, own, depth, n_parts, *refs):
    parts, outs, grad = refs[:n_parts], refs[n_parts:-1], refs[-1]
    shared = sum_rows(parts, 0, depth).astype(BF16) if depth else None
    grad[...] = sum_rows(parts, depth + NORM_ROWS, grad.shape[0])
    put_shares(axis, weight, own, shared, sum_norm(parts, depth), grad, outs)


def first_digit(axis):
    return next(digits(lax.axis_size(axis)))


def messages(depth, rows, rank, radix, dtype):
    return [((depth + NORM_ROWS + rows // radix, rank), dtype)] * radix


def sum_shares(sent, axis, own, depth, beside=None):
    rank = sent[0].shape[1]
    parts = None
    for weight, radix in digits(lax.axis_size(axis)):
        if parts is not None:
            held = parts[0].shape[0] - depth - NORM_ROWS
            sent = call(
                functools.partial(next_shares_kernel, axis, weight, own, depth, len(parts)),
                messages(depth, held, rank, radix, sent[0].dtype),
                *parts,
                scratch=[pltpu.VMEM((held, rank), F32)],
            )
            if beside is not None:
                sent, _ = lax.optimization_barrier((sent, beside))
        got = [swap(x, axis, weight, q) for q, x in zip(turns(radix)[1:], sent[1:])]
        parts = [sent[0]] + got
    return parts


def last_a_kernel(n_col, *refs):
    cols, refs = refs[:n_col], refs[n_col:]
    a_ref, c_ref, out_a = refs
    own_i = out_a.shape[0]
    norm_c = squares(c_ref[...].astype(BF16))
    step_a = scaling / (sum_norm(cols, 0) * norm_c + epsilon)
    at_i = pl.ds(pl.multiple_of(lax.axis_index("col") * own_i, own_i), own_i)
    out_a[...] = damping * a_ref[at_i] + step_a * sum_rows(cols, NORM_ROWS, own_i)


def half_kernel(n_row, n_col, *refs):
    rows, refs = refs[:n_row], refs[n_row:]
    cols, (half, step_c) = refs[:n_col], refs[n_col:]
    half[...] = sum_rows(rows, 0, half.shape[0])
    norm = sum_norm(rows, half.shape[0]) * sum_norm(cols, 0)
    step_c[...] = jnp.broadcast_to(scaling / (norm + epsilon), step_c.shape)


def last_b_kernel(n_row, *refs):
    rows, (b_ref, c_ref, out_b) = refs[:n_row], refs[n_row:]
    depth, own_j = c_ref.shape[0] // 2, out_b.shape[0]
    norm_c = squares(c_ref[...].astype(BF16))
    step_b = scaling / (sum_norm(rows, depth) * norm_c + epsilon)
    at_j = pl.ds(pl.multiple_of(lax.axis_index("row") * own_j, own_j), own_j)
    out_b[...] = damping * b_ref[at_j] + step_b * sum_rows(rows, depth + NORM_ROWS, own_j)


def last_c_kernel(half, got, step_c, c_ref, out_c):
    rows = half.shape[0]
    for ref, other in ((half, False), (got, True)):
        at = core_rows(rows, other)
        out_c[at] = damping * c_ref[at] + step_c[0:1] * ref[...]


def local(tensor, factor_a, factor_b, factor_c):
    rows_i, rows_j, depth = tensor.shape
    rank = factor_a.shape[1]
    held_a, held_b, c = hold(factor_a, factor_b, factor_c)
    b = gather(factor_b, held_b, "row")
    a = gather(held_a, held_a, "col")

    kept = kept_shapes(tensor, rank)
    grad_b, low, high = call(
        first_b_kernel, [(b.shape, F32)] + kept, tensor, a, c, flops=2 * tensor.size * rank
    )
    (to_row,) = call(
        first_c_kernel,
        [((rows_j + depth + NORM_ROWS, rank), BF16)],
        tensor, a, b, c, grad_b,
        scratch=[pltpu.VMEM(c.shape, F32)],
        flops=2 * tensor.size * rank,
    )
    (to_col,) = call(
        first_a_kernel,
        [((rows_i + NORM_ROWS, rank), BF16)],
        low, high, a, b, c,
        scratch=[pltpu.VMEM(a.shape, F32)],
        flops=tensor.size * rank,
    )
    rows = sum_parts(to_row, "row", rows_j + depth, high_first=True)
    cols = sum_parts(to_col, "col", rows_i)
    a, gram_a = call(
        functools.partial(new_a_kernel, len(cols)),
        [(a.shape, F32), ((rank, rank), F32)],
        *cols, a, c,
    )
    b, part_c, step_c = call(
        functools.partial(middle_kernel, len(rows), len(cols)),
        [(b.shape, F32), (c.shape, BF16), ((8, rank), F32)],
        *rows, *cols, b, c,
    )

    parts = sum_parts(part_c, "col")
    sum_t, gram_ab = call(
        second_c_kernel,
        [(c.shape, F32), ((rank, rank), F32)],
        tensor, a, b, gram_a,
        flops=2 * tensor.size * rank,
    )
    c, to_col = call(
        functools.partial(second_model_kernel, len(parts)),
        [(c.shape, F32), (c.shape, BF16)],
        *parts, step_c, c, sum_t, gram_ab,
    )
    parts = sum_parts(to_col, "col")
    grad_b, low, high = call(
        second_b_kernel, [(b.shape, F32)] + kept, tensor, a, b, c, gram_a, flops=2 * tensor.size * rank
    )
    weight, radix = first_digit("row")
    to_row = call(
        functools.partial(shares_kernel, len(parts), factor_b.shape[0], weight),
        messages(depth // 2, rows_j, rank, radix, BF16),
        *parts, a, grad_b,
        scratch=[pltpu.VMEM(c.shape, F32)],
    )
    weight, radix = first_digit("col")
    to_col = call(
        functools.partial(second_a_kernel, weight, factor_a.shape[0]),
        messages(0, rows_i, rank, radix, F32),
        low, high, a, b, c,
        scratch=[pltpu.VMEM((rows_i, rank), F32)],
        flops=tensor.size * rank,
    )
    rows = sum_shares(to_row, "row", factor_b.shape[0], depth // 2, to_col)
    cols = sum_shares(to_col, "col", factor_a.shape[0], 0)
    (out_a,) = call(
        functools.partial(last_a_kernel, len(cols)),
        [(factor_a.shape, F32)],
        *cols, a, c,
        hbm_out=True,
    )
    half, step_c = call(
        functools.partial(half_kernel, len(rows), len(cols)),
        [((depth // 2, rank), F32), ((8, rank), F32)],
        *rows, *cols,
    )
    got = swap(half, "col", 1, 1)
    (out_b,) = call(
        functools.partial(last_b_kernel, len(rows)),
        [(factor_b.shape, F32)],
        *rows, b, c,
        hbm_out=True,
    )
    (out_c,) = call(last_c_kernel, [(c.shape, F32)], half, got, step_c, c, hbm_out=True)
    return (out_a, out_b, out_c)


def solution(mesh):
    return jax.shard_map(
        local,
        mesh=mesh,
        in_specs=(P("row", "col", None), P(("row", "col"), None), P(("col", "row"), None), P()),
        out_specs=(P(("row", "col"), None), P(("col", "row"), None), P()),
        check_vma=False,
    )
```

```python
import functools

import jax
import jax.numpy as jnp
from jax import lax
from jax.experimental import pallas as pl
from jax.experimental.pallas import tpu as pltpu
from jax.sharding import PartitionSpec as P

F32 = jnp.float32
BF16 = jnp.bfloat16
NORM_ROWS = 16
VMEM_LIMIT = 4 << 20
HOLD_FLOPS = 5 * 10**9
PLACE_FLOPS = 2 * 10**9


damping = 0.9
scaling = 0.25
epsilon = 1e-06


def vmem(x):
    return pltpu.with_memory_space_constraint(x, pltpu.VMEM)


def call(body, outs, *operands, scratch=(), hbm_out=False, flops=0):
    whole = pl.BlockSpec(memory_space=pltpu.VMEM)
    place = jax.ShapeDtypeStruct if hbm_out else pltpu.VMEM
    return pl.pallas_call(
        body,
        in_specs=[whole] * len(operands),
        out_specs=[whole] * len(outs),
        out_shape=[place(s, d) for s, d in outs],
        scratch_shapes=scratch,
        cost_estimate=pl.CostEstimate(flops=flops, bytes_accessed=0, transcendentals=0),
        compiler_params=pltpu.CompilerParams(vmem_limit_bytes=VMEM_LIMIT),
    )(*[vmem(x) for x in operands])


def divisor(n, most):
    return next(g for g in (256, 128, 64, 32, 16, 8, 4, 2) if g <= most and n % g == 0)


def dot(x, y):
    return jnp.dot(x, y, preferred_element_type=F32)


def dot_rows(x, y):
    return lax.dot_general(x, y, (((0,), (0,)), ((), ())), preferred_element_type=F32)


def gram(x16):
    return dot_rows(x16, x16)


def dot_wide(x16, y):
    high = y.astype(BF16)
    low = (y - high.astype(F32)).astype(BF16)
    return dot(x16, high) + dot(x16, low)


def put_norm(ref, start, norm):
    high = norm.astype(BF16).astype(F32)
    rest = norm - high
    mid = rest.astype(BF16).astype(F32)
    low = rest - mid
    rows = jnp.concatenate([high, mid, low, jnp.zeros((NORM_ROWS - 3, norm.shape[1]), F32)], 0)
    ref[start : start + NORM_ROWS] = rows.astype(ref.dtype)


def get_norm(ref, start):
    rows = ref[start : start + NORM_ROWS].astype(F32)
    return rows[0:1] + rows[1:2] + rows[2:3]


def squares(x16):
    return jnp.sum(jnp.square(x16.astype(F32)), axis=0, keepdims=True)


def tree(parts):
    while len(parts) > 1:
        parts = [parts[q] + parts[q + 1] for q in range(0, len(parts), 2)]
    return parts[0]


def sum_rows(refs, start, rows):
    return tree([r[start : start + rows].astype(F32) for r in refs])


def sum_norm(refs, start):
    return tree([get_norm(r, start) for r in refs])


def digits(n):
    weight = 1
    while weight < n:
        radix = 4 if (n // weight) % 4 == 0 else 2
        yield weight, radix
        weight *= radix


def digit_of(axis, weight, radix):
    return lax.rem(lax.div(lax.axis_index(axis), weight), radix)


def swap(x, axis, weight, q):
    return lax.ppermute(x, axis, [(i, i ^ (q * weight)) for i in range(lax.axis_size(axis))])


def turns(radix):
    return [0] + list(range(radix - 1, 0, -1))


def twice(c16):
    zero = jnp.zeros_like(c16)
    return jnp.concatenate(
        [jnp.concatenate([c16, zero], 1), jnp.concatenate([zero, c16], 1)], 0
    )


def place_kernel(axis, weight, *refs):
    *ins, out = refs
    rows = ins[0].shape[0]
    digit = digit_of(axis, weight, len(ins))
    for q, ref in zip(turns(len(ins)), ins):
        out[pl.ds(pl.multiple_of((digit ^ q) * rows, rows), rows)] = ref[...]


def gather_digit(x, own, axis, weight, radix):
    got = [swap(x, axis, weight, q) for q in turns(radix)[1:]]
    (x,) = call(
        functools.partial(place_kernel, axis, weight),
        [((x.shape[0] * radix, x.shape[1]), x.dtype)],
        own, *got,
        flops=PLACE_FLOPS,
    )
    return x


def gather(x, own, axis):
    for weight, radix in digits(lax.axis_size(axis)):
        x = own = gather_digit(x, own, axis, weight, radix)
    return x


def hold_kernel(*refs):
    half = len(refs) // 2
    for ref, out in zip(refs[:half], refs[half:]):
        out[...] = ref[...]


def hold(*arrays):
    whole = pl.BlockSpec(memory_space=pltpu.VMEM)
    return pl.pallas_call(
        hold_kernel,
        out_specs=[whole] * len(arrays),
        out_shape=[pltpu.VMEM(x.shape, x.dtype) for x in arrays],
        cost_estimate=pl.CostEstimate(flops=HOLD_FLOPS, bytes_accessed=0, transcendentals=0),
    )(*[pltpu.with_memory_space_constraint(x, pltpu.HBM) for x in arrays])


def add_kernel(norm_at, *refs):
    *ins, out = refs
    out[...] = sum_rows(ins, 0, out.shape[0]).astype(BF16)
    if norm_at is not None:
        put_norm(out, norm_at, sum_norm(ins, norm_at))


def sum_parts(x, axis, norm_at=None, high_first=False):
    parts = [x]
    order = list(digits(lax.axis_size(axis)))
    for weight, radix in reversed(order) if high_first else order:
        if len(parts) > 1:
            (x,) = call(functools.partial(add_kernel, norm_at), [(x.shape, BF16)], *parts)
        parts = [x] + [swap(x, axis, weight, q) for q in turns(radix)[1:]]
    return parts


def sum_c(t_ref, a_ref, b16, acc):
    rows_i, rows_j, depth = t_ref.shape
    group = divisor(rows_i, 256)
    acc[...] = jnp.zeros_like(acc)

    def step(g, carry):
        at = pl.ds(pl.multiple_of(g * group, group), group)
        a16 = a_ref[at].astype(BF16)
        pairs = jnp.concatenate([a16[q : q + 1] * b16 for q in range(group)], 0)
        acc[...] += dot_rows(t_ref[at].reshape(group * rows_j, depth), pairs)
        return carry

    lax.fori_loop(0, rows_i // group, step, 0)


def sum_b(t_ref, a_ref, c16, acc, low, high):
    rows_i, rows_j, depth = t_ref.shape
    rank = c16.shape[1]
    half = rows_i // 2
    group = divisor(half, 128)
    pair_c = twice(c16)
    acc[...] = jnp.zeros_like(acc)

    def step(g, carry):
        first = pl.multiple_of(g * group, group)
        left, right = t_ref[pl.ds(first, group)], t_ref[pl.ds(half + first, group)]
        a_left = a_ref[pl.ds(first, group)].astype(BF16).astype(F32)
        a_right = a_ref[pl.ds(half + first, group)].astype(BF16).astype(F32)
        total = acc[...]
        for q in range(group):
            along = dot(jnp.concatenate([left[q], right[q]], 1), pair_c)
            for part, kept, a32 in ((along[:, :rank], low, a_left), (along[:, rank:], high, a_right)):
                kept[first + q] = part
                total = total + part * a32[q : q + 1]
        acc[...] = total
        return carry

    lax.fori_loop(0, half // group, step, 0)


def sum_a(low, high, b16, acc):
    half = low.shape[0]
    group = divisor(half, 128)
    b32 = b16.astype(F32)

    def step(g, carry):
        first = pl.multiple_of(g * group, group)
        for start, kept in ((first, low), (half + first, high)):
            sums = [jnp.sum(kept[first + q] * b32, axis=0, keepdims=True) for q in range(group)]
            acc[pl.ds(start, group)] = jnp.concatenate(sums, 0)
        return carry

    lax.fori_loop(0, half // group, step, 0)


def kept_shapes(tensor, rank):
    rows_i, rows_j, _ = tensor.shape
    return [((rows_i // 2, rows_j, rank), F32)] * 2


def first_b_kernel(t_ref, a_ref, c_ref, acc, low, high):
    sum_b(t_ref, a_ref, c_ref[...].astype(BF16), acc, low, high)


def first_c_kernel(t_ref, a_ref, b_ref, c_ref, acc_b, row_ref, acc_c):
    rows_j, depth = b_ref.shape[0], c_ref.shape[0]
    a16 = a_ref[...].astype(BF16)
    b16 = b_ref[...].astype(BF16)
    c16 = c_ref[...].astype(BF16)
    gram_a, gram_b, gram_c = gram(a16), gram(b16), gram(c16)
    sum_c(t_ref, a_ref, b16, acc_c)
    row_ref[:rows_j] = (acc_b[...] - dot_wide(b16, gram_a * gram_c)).astype(BF16)
    row_ref[rows_j : rows_j + depth] = (acc_c[...] - dot_wide(c16, gram_a * gram_b)).astype(BF16)
    put_norm(row_ref, rows_j + depth, squares(a16))


def first_a_kernel(low, high, a_ref, b_ref, c_ref, col_ref, acc_a):
    rows_i = a_ref.shape[0]
    b16 = b_ref[...].astype(BF16)
    sum_a(low, high, b16, acc_a)
    model = dot_wide(a_ref[...].astype(BF16), gram(b16) * gram(c_ref[...].astype(BF16)))
    col_ref[:rows_i] = (acc_a[...] - model).astype(BF16)
    put_norm(col_ref, rows_i, squares(b16))


def new_a_kernel(n_col, *refs):
    cols, refs = refs[:n_col], refs[n_col:]
    a_ref, c_ref, new_a, gram_a = refs
    rows_i = a_ref.shape[0]
    norm_c = squares(c_ref[...].astype(BF16))
    step_a = scaling / (sum_norm(cols, rows_i) * norm_c + epsilon)
    a2 = damping * a_ref[...] + step_a * sum_rows(cols, 0, rows_i)
    new_a[...] = a2
    gram_a[...] = gram(a2.astype(BF16))


def middle_kernel(n_row, n_col, *refs):
    rows, refs = refs[:n_row], refs[n_row:]
    cols, refs = refs[:n_col], refs[n_col:]
    b_ref, c_ref, new_b, part_c, step_c = refs
    rows_j, depth = b_ref.shape[0], c_ref.shape[0]
    norm_a = sum_norm(rows, rows_j + depth)
    norm_b = sum_norm(cols, cols[0].shape[0] - NORM_ROWS)
    norm_c = squares(c_ref[...].astype(BF16))
    step_b = scaling / (norm_a * norm_c + epsilon)
    new_b[...] = damping * b_ref[...] + step_b * sum_rows(rows, 0, rows_j)
    part_c[...] = sum_rows(rows, rows_j, depth).astype(BF16)
    step_c[...] = jnp.broadcast_to(scaling / (norm_a * norm_b + epsilon), step_c.shape)


def second_c_kernel(t_ref, a_ref, b_ref, gram_a, sum_ref, gram_ref):
    b16 = b_ref[...].astype(BF16)
    sum_c(t_ref, a_ref, b16, sum_ref)
    gram_ref[...] = gram_a[...] * gram(b16)


def second_model_kernel(n_col, *refs):
    parts, refs = refs[:n_col], refs[n_col:]
    step_ref, c_ref, sum_ref, gram_ref, new_c, out_ref = refs
    c2 = damping * c_ref[...] + step_ref[0:1] * sum_rows(parts, 0, c_ref.shape[0])
    new_c[...] = c2
    out_ref[...] = (sum_ref[...] - dot_wide(c2.astype(BF16), gram_ref[...])).astype(BF16)


def second_b_kernel(t_ref, a_ref, b_ref, c_ref, gram_a, grad_b, low, high):
    c16 = c_ref[...].astype(BF16)
    model = dot_wide(b_ref[...].astype(BF16), gram_a[...] * gram(c16))
    sum_b(t_ref, a_ref, c16, grad_b, low, high)
    grad_b[...] -= model


def second_a_kernel(weight, own_i, low, high, a_ref, b_ref, c_ref, *refs):
    *outs, acc_a = refs
    b16 = b_ref[...].astype(BF16)
    sum_a(low, high, b16, acc_a)
    acc_a[...] -= dot_wide(a_ref[...].astype(BF16), gram(b16) * gram(c_ref[...].astype(BF16)))
    put_shares("col", weight, own_i, None, squares(b16), acc_a, outs)


def put_shares(axis, weight, own, shared, norm, grad, outs):
    radix = len(outs)
    depth = 0 if shared is None else shared.shape[0]
    blocks = grad.shape[0] // own
    digit = digit_of(axis, weight, radix)
    for q, out in zip(turns(radix), outs):
        if depth:
            out[:depth] = shared
        put_norm(out, depth, norm)
        first = [(high * radix + (digit ^ q)) * own for high in range(blocks // radix)]
        rows = [grad[pl.ds(pl.multiple_of(at, own), own)] for at in first]
        out[depth + NORM_ROWS :] = jnp.concatenate(rows, 0).astype(out.dtype)


def shares_kernel(n_col, own_j, weight, *refs):
    parts, refs = refs[:n_col], refs[n_col:]
    a_ref, grad_b, outs = refs[0], refs[1], refs[2:]
    shared = sum_rows(parts, 0, parts[0].shape[0]).astype(BF16)
    put_shares("row", weight, own_j, shared, squares(a_ref[...].astype(BF16)), grad_b, outs)


def next_shares_kernel(axis, weight, own, depth, n_parts, *refs):
    parts, outs, grad = refs[:n_parts], refs[n_parts:-1], refs[-1]
    shared = sum_rows(parts, 0, depth).astype(BF16) if depth else None
    grad[...] = sum_rows(parts, depth + NORM_ROWS, grad.shape[0])
    put_shares(axis, weight, own, shared, sum_norm(parts, depth), grad, outs)


def first_digit(axis):
    return next(digits(lax.axis_size(axis)))


def messages(depth, rows, rank, radix, dtype):
    return [((depth + NORM_ROWS + rows // radix, rank), dtype)] * radix


def sum_shares(sent, axis, own, depth, beside=None):
    rank = sent[0].shape[1]
    parts = None
    for weight, radix in digits(lax.axis_size(axis)):
        if parts is not None:
            held = parts[0].shape[0] - depth - NORM_ROWS
            sent = call(
                functools.partial(next_shares_kernel, axis, weight, own, depth, len(parts)),
                messages(depth, held, rank, radix, sent[0].dtype),
                *parts,
                scratch=[pltpu.VMEM((held, rank), F32)],
            )
            if beside is not None:
                sent, _ = lax.optimization_barrier((sent, beside))
        got = [swap(x, axis, weight, q) for q, x in zip(turns(radix)[1:], sent[1:])]
        parts = [sent[0]] + got
    return parts


def last_a_kernel(n_col, *refs):
    cols, refs = refs[:n_col], refs[n_col:]
    a_ref, c_ref, out_a = refs
    own_i = out_a.shape[0]
    norm_c = squares(c_ref[...].astype(BF16))
    step_a = scaling / (sum_norm(cols, 0) * norm_c + epsilon)
    at_i = pl.ds(pl.multiple_of(lax.axis_index("col") * own_i, own_i), own_i)
    out_a[...] = damping * a_ref[at_i] + step_a * sum_rows(cols, NORM_ROWS, own_i)


def last_kernel(n_row, n_col, *refs):
    rows, refs = refs[:n_row], refs[n_row:]
    cols, refs = refs[:n_col], refs[n_col:]
    b_ref, c_ref, out_b, out_c = refs
    depth = c_ref.shape[0]
    own_j = out_b.shape[0]
    norm_a = sum_norm(rows, depth)
    norm_b = sum_norm(cols, 0)
    norm_c = squares(c_ref[...].astype(BF16))
    step_b = scaling / (norm_a * norm_c + epsilon)
    step_c = scaling / (norm_a * norm_b + epsilon)
    at_j = pl.ds(pl.multiple_of(lax.axis_index("row") * own_j, own_j), own_j)
    out_b[...] = damping * b_ref[at_j] + step_b * sum_rows(rows, depth + NORM_ROWS, own_j)
    out_c[...] = damping * c_ref[...] + step_c * sum_rows(rows, 0, depth)


def local(tensor, factor_a, factor_b, factor_c):
    rows_i, rows_j, depth = tensor.shape
    rank = factor_a.shape[1]
    held_a, held_b, c = hold(factor_a, factor_b, factor_c)
    b = gather(factor_b, held_b, "row")
    a = gather(held_a, held_a, "col")

    kept = kept_shapes(tensor, rank)
    grad_b, low, high = call(
        first_b_kernel, [(b.shape, F32)] + kept, tensor, a, c, flops=2 * tensor.size * rank
    )
    (to_row,) = call(
        first_c_kernel,
        [((rows_j + depth + NORM_ROWS, rank), BF16)],
        tensor, a, b, c, grad_b,
        scratch=[pltpu.VMEM(c.shape, F32)],
        flops=2 * tensor.size * rank,
    )
    (to_col,) = call(
        first_a_kernel,
        [((rows_i + NORM_ROWS, rank), BF16)],
        low, high, a, b, c,
        scratch=[pltpu.VMEM(a.shape, F32)],
        flops=tensor.size * rank,
    )
    rows = sum_parts(to_row, "row", rows_j + depth, high_first=True)
    cols = sum_parts(to_col, "col", rows_i)
    a, gram_a = call(
        functools.partial(new_a_kernel, len(cols)),
        [(a.shape, F32), ((rank, rank), F32)],
        *cols, a, c,
    )
    b, part_c, step_c = call(
        functools.partial(middle_kernel, len(rows), len(cols)),
        [(b.shape, F32), (c.shape, BF16), ((8, rank), F32)],
        *rows, *cols, b, c,
    )

    parts = sum_parts(part_c, "col")
    sum_t, gram_ab = call(
        second_c_kernel,
        [(c.shape, F32), ((rank, rank), F32)],
        tensor, a, b, gram_a,
        flops=2 * tensor.size * rank,
    )
    c, to_col = call(
        functools.partial(second_model_kernel, len(parts)),
        [(c.shape, F32), (c.shape, BF16)],
        *parts, step_c, c, sum_t, gram_ab,
    )
    parts = sum_parts(to_col, "col")
    grad_b, low, high = call(
        second_b_kernel, [(b.shape, F32)] + kept, tensor, a, b, c, gram_a, flops=2 * tensor.size * rank
    )
    weight, radix = first_digit("row")
    to_row = call(
        functools.partial(shares_kernel, len(parts), factor_b.shape[0], weight),
        messages(depth, rows_j, rank, radix, BF16),
        *parts, a, grad_b,
    )
    weight, radix = first_digit("col")
    to_col = call(
        functools.partial(second_a_kernel, weight, factor_a.shape[0]),
        messages(0, rows_i, rank, radix, F32),
        low, high, a, b, c,
        scratch=[pltpu.VMEM((rows_i, rank), F32)],
        flops=tensor.size * rank,
    )
    rows = sum_shares(to_row, "row", factor_b.shape[0], depth, to_col)
    cols = sum_shares(to_col, "col", factor_a.shape[0], 0)
    (out_a,) = call(
        functools.partial(last_a_kernel, len(cols)),
        [(factor_a.shape, F32)],
        *cols, a, c,
        hbm_out=True,
    )
    out_b, out_c = call(
        functools.partial(last_kernel, len(rows), len(cols)),
        [(factor_b.shape, F32), (c.shape, F32)],
        *rows, *cols, b, c,
        hbm_out=True,
    )
    return (out_a, out_b, out_c)


def solution(mesh):
    return jax.shard_map(
        local,
        mesh=mesh,
        in_specs=(P("row", "col", None), P(("row", "col"), None), P(("col", "row"), None), P()),
        out_specs=(P(("row", "col"), None), P(("col", "row"), None), P()),
        check_vma=False,
    )
```
